32 devices in a mesh: own: 4 (over z), img: 8 (over y, x, core).
Axes of the slice: x: 2, y: 2, z: 4, core: 2. Of those that a mesh axis runs over, the one named last changes fastest.
Arguments:
- mask_field: bfloat16 [4096, 4096], P('own', 'img'), may hold values from -1 to 1
- target_field: bfloat16 [4096, 4096], P('own', 'img'), may hold values from 0 to 1
- occupancy: int32 [8, 8], replicated, may hold values 0 or 1
- kernels: float32 [2, 24, 32, 32], replicated, may hold values from -9 to 9
- weights: float32 [24], replicated, may hold values from 0.01 to 0.3
Outputs:
- gradient: float32 [4096, 4096], P('own', 'img')
The draws below stay inside these ranges and needn't reach their ends.
All inputs are finite; a program needn't handle non-finite values.
Results may differ from the reference program's by a relative error of at most 0.0072.
Values may be sent and summed in bfloat16 or wider, within the bound.
A program may use at most 64 MiB of HBM per device.

```python
import math
import jax
import jax.numpy as jnp
from jax import lax

TILE = 512
AMBIT = 64
FREQ = 32
KERNELS = 24
PAD = 640
GY = 8
GX = 8
NY = 4096
NX = 4096


def with_ends(drawn, stream_key, smallest, largest):
    longest = drawn.shape.index(max(drawn.shape))
    spots = []
    for shift in (0, 1):
        where = [jax.random.randint(jax.random.fold_in(stream_key, axis), (), 0, length) for axis, length in enumerate(drawn.shape)]
        where[longest] = (where[longest] + shift) % drawn.shape[longest]
        spots.append(tuple(where))
    return drawn.at[spots[0]].set(smallest).at[spots[1]].set(largest)


def block_levels(rng, dims, pieces, low, largest):
    loudness = 1.0
    for dim, shards_of in pieces:
        steps = jax.random.uniform(jax.random.fold_in(jax.random.fold_in(rng, 6), dim), (shards_of,), jnp.float32, low / len(pieces), largest / len(pieces))
        loudness = loudness * jnp.repeat(jnp.exp(steps), dims[dim] // shards_of).reshape((-1,) + (1,) * (len(dims) - 1 - dim))
    return loudness


def normal_values(rng, extent, deviation, most, kind=jnp.bfloat16):
    drawn = deviation * jax.random.normal(rng, extent, jnp.float32)
    return jnp.clip(drawn, min=-most, max=most).astype(kind)


def setup_inputs(seed: int = 0) -> dict:
    key_of = jax.random.split(jax.random.key(seed), 6)
    mask_field = jnp.clip(jax.random.uniform(key_of[0], (NY, NX), jnp.float32, -1.0, 1.0) * block_levels(key_of[0], (NY, NX), ((0, 4), (1, 8)), -0.4, 0.0), -1.0, 1.0).astype(jnp.bfloat16)
    target_field = jnp.clip(1.0 * jax.random.uniform(key_of[1], (NY, NX), jnp.float32) ** block_levels(key_of[1], (NY, NX), ((0, 4), (1, 8)), -0.2, 0.2), 0.0, 1.0).astype(jnp.bfloat16)
    occupancy = with_ends((jax.random.randint(key_of[2], (GY, GX), 0, 5) < 2).astype(jnp.int32), jax.random.fold_in(key_of[2], 1), 0, 1)
    kernels = normal_values(key_of[3], (2, KERNELS, FREQ, FREQ), 1.5, 9.0, jnp.float32)
    weights = jnp.clip(jnp.exp(jax.random.uniform(key_of[4], (KERNELS,), jnp.float32, math.log(0.01), math.log(0.3))), 0.01, 0.3)
    return {"mask_field": mask_field, "target_field": target_field, "occupancy": occupancy, "kernels": kernels, "weights": weights}


STEEP = 2.0
THRESHOLD = 1.5
GAMMA = 0.25

def mixed_dot(left, right):
    return jnp.dot(left, right, preferred_element_type=jnp.float32)

def exact_dot(left, right):
    return jnp.dot(left, right, precision=lax.Precision.HIGHEST, preferred_element_type=jnp.float32)

def dft_tables(padded_len, core_len, ambit_len, freq_count):
    freqs = jnp.arange(freq_count, dtype=jnp.int32) - freq_count // 2
    pixels = jnp.arange(padded_len, dtype=jnp.int32)
    phase = jnp.mod(freqs[:, None] * pixels[None, :], padded_len).astype(jnp.float32) * (2.0 * math.pi / padded_len)
    fwd_cos = (jnp.cos(phase) / math.sqrt(padded_len)).astype(jnp.bfloat16)
    fwd_sin = (-jnp.sin(phase) / math.sqrt(padded_len)).astype(jnp.bfloat16)
    out_rows = jnp.arange(core_len, dtype=jnp.int32) + ambit_len
    back_phase = jnp.mod(out_rows[:, None] * freqs[None, :], padded_len).astype(jnp.float32) * (2.0 * math.pi / padded_len)
    inv_cos = (jnp.cos(back_phase) / math.sqrt(freq_count)).astype(jnp.bfloat16)
    inv_sin = (jnp.sin(back_phase) / math.sqrt(freq_count)).astype(jnp.bfloat16)
    return (fwd_cos, fwd_sin, inv_cos, inv_sin)

def tile_gradient(padded_tile, target_tile, kernels, weights, tables):
    fwd_cos, fwd_sin, inv_cos, inv_sin = tables
    back_cos = inv_cos.astype(jnp.float32)
    back_sin = inv_sin.astype(jnp.float32)
    upper_re = mixed_dot(fwd_cos, padded_tile).astype(jnp.bfloat16)
    upper_im = mixed_dot(fwd_sin, padded_tile).astype(jnp.bfloat16)
    spec_re = mixed_dot(upper_re, fwd_cos.T) - mixed_dot(upper_im, fwd_sin.T)
    spec_im = mixed_dot(upper_re, fwd_sin.T) + mixed_dot(upper_im, fwd_cos.T)

    def field(which):
        kern_re = kernels[0, which]
        kern_im = kernels[1, which]
        prod_re = kern_re * spec_re - kern_im * spec_im
        prod_im = kern_re * spec_im + kern_im * spec_re
        half_re = (exact_dot(prod_re, back_cos.T) - exact_dot(prod_im, back_sin.T)).astype(jnp.bfloat16)
        half_im = (exact_dot(prod_re, back_sin.T) + exact_dot(prod_im, back_cos.T)).astype(jnp.bfloat16)
        field_re = mixed_dot(inv_cos, half_re) - mixed_dot(inv_sin, half_im)
        field_im = mixed_dot(inv_cos, half_im) + mixed_dot(inv_sin, half_re)
        return (field_re, field_im)

    def add_intensity(which, total):
        field_re, field_im = field(which)
        return total + weights[which] * (field_re * field_re + field_im * field_im)
    intensity = lax.fori_loop(0, KERNELS, add_intensity, jnp.zeros((TILE, TILE), jnp.float32))
    resist = jax.nn.sigmoid(STEEP * (intensity - THRESHOLD))
    sens = 2.0 * (resist - target_tile.astype(jnp.float32)) * STEEP * resist * (1.0 - resist)

    def add_adjoint(which, spec_grad):
        kern_re = kernels[0, which]
        kern_im = kernels[1, which]
        field_re, field_im = field(which)
        factor = 2.0 * weights[which] * sens
        cot_re = (factor * field_re).astype(jnp.bfloat16)
        cot_im = (factor * field_im).astype(jnp.bfloat16)
        dp_re = mixed_dot(inv_cos.T, cot_re) + mixed_dot(inv_sin.T, cot_im)
        dp_im = mixed_dot(inv_cos.T, cot_im) - mixed_dot(inv_sin.T, cot_re)
        ds_re = exact_dot(dp_re, back_cos) + exact_dot(dp_im, back_sin)
        ds_im = exact_dot(dp_im, back_cos) - exact_dot(dp_re, back_sin)
        grad_re, grad_im = spec_grad
        return (grad_re + kern_re * ds_re + kern_im * ds_im, grad_im + kern_re * ds_im - kern_im * ds_re)
    zero_spec = jnp.zeros((FREQ, FREQ), jnp.float32)
    grad_re, grad_im = lax.fori_loop(0, KERNELS, add_adjoint, (zero_spec, zero_spec))
    fwd_cos_wide = fwd_cos.astype(jnp.float32)
    fwd_sin_wide = fwd_sin.astype(jnp.float32)
    du_re = (exact_dot(grad_re, fwd_cos_wide) + exact_dot(grad_im, fwd_sin_wide)).astype(jnp.bfloat16)
    du_im = (exact_dot(grad_im, fwd_cos_wide) - exact_dot(grad_re, fwd_sin_wide)).astype(jnp.bfloat16)
    return mixed_dot(fwd_cos.T, du_re) + mixed_dot(fwd_sin.T, du_im)

def reference(mask_field, target_field, occupancy, kernels, weights):
    tables = dft_tables(PAD, TILE, AMBIT, FREQ)
    padded_field = jnp.pad(mask_field, AMBIT)
    total = jnp.zeros((NY + 2 * AMBIT, NX + 2 * AMBIT), jnp.float32)
    blank = jnp.zeros((PAD, PAD), jnp.float32)

    def visit(total, position):
        row_tile = position // GX
        col_tile = position % GX
        top = (row_tile * TILE).astype(jnp.int32)
        left = (col_tile * TILE).astype(jnp.int32)
        window = lax.dynamic_slice(padded_field, (top, left), (PAD, PAD))
        wanted = lax.dynamic_slice(target_field, (top, left), (TILE, TILE))
        flag = occupancy[row_tile, col_tile]
        contrib = lax.cond(flag > 0, lambda: tile_gradient(window, wanted, kernels, weights, tables), lambda: blank)
        contrib = lax.optimization_barrier(contrib.astype(jnp.bfloat16)).astype(jnp.float32)
        current = lax.dynamic_slice(total, (top, left), (PAD, PAD))
        return (lax.dynamic_update_slice(total, current + contrib, (top, left)), None)
    total, unused = lax.scan(visit, total, jnp.arange(GY * GX, dtype=jnp.int32))
    values = mask_field.astype(jnp.float32)
    penalty = GAMMA * 4.0 * values * (values * values - 1.0)
    return total[AMBIT:AMBIT + NY, AMBIT:AMBIT + NX] + penalty
```

```python
import math

import jax
import jax.numpy as jnp
import numpy as np
from jax import lax
from jax.experimental import pallas as pl
from jax.experimental.pallas import tpu as pltpu
from jax.sharding import PartitionSpec as P

TILE = 512
AMBIT = 64
FREQ = 32
KERNELS = 24
PAD = 640
STEEP = 2.0
THRESHOLD = 1.5
GAMMA = 0.25
GROUP = 8
BH = 256
BW = 128
BATCH = 4


def tables():
    freqs = np.arange(FREQ) - FREQ // 2
    turn = np.float32(2.0 * math.pi / PAD)
    phase = ((freqs[:, None] * np.arange(PAD)[None, :]) % PAD).astype(np.float32) * turn
    back = (((np.arange(TILE) + AMBIT)[:, None] * freqs[None, :]) % PAD).astype(np.float32) * turn
    bf = lambda a: np.asarray(a, np.float32).astype(jnp.bfloat16)
    return (
        bf(np.cos(phase) / np.float32(math.sqrt(PAD))),
        bf(-np.sin(phase) / np.float32(math.sqrt(PAD))),
        bf(np.cos(back) / np.float32(math.sqrt(FREQ))),
        bf(np.sin(back) / np.float32(math.sqrt(FREQ))),
    )


FC, FS, HC, HS = tables()
FORWARD = np.concatenate([FC, FS], 0)
INVERSE = np.concatenate([HC, HS], 1)


def spread(count):
    length = count * TILE
    out = np.zeros((count + 2, 2 * FREQ, length), jnp.bfloat16)
    for tile in range(-1, count + 1):
        start = tile * TILE - AMBIT
        low, high = max(start, 0), min(start + PAD, length)
        out[tile + 1, :, low:high] = FORWARD[:, low - start : high - start]
    return out.reshape(-1, length)


def column_tables():
    there, back = [], []
    for block in range(TILE // BW):
        c = HC[block * BW : (block + 1) * BW].astype(np.float32)
        s = HS[block * BW : (block + 1) * BW].astype(np.float32)
        one = np.block([[c.T, s.T], [-s.T, c.T]])
        there.append(np.concatenate([one, one], 0))
        adj = np.concatenate([np.block([[c, -s], [s, c]]), np.block([[-s, -c], [c, -s]])], 1)
        back.append(np.concatenate([adj, adj], 0))
    return np.stack(there).astype(jnp.bfloat16), np.stack(back).astype(jnp.bfloat16)


THERE, BACK = column_tables()


def mixed_dot(left, right):
    return jnp.dot(left, right, preferred_element_type=jnp.float32)


def two_parts(value):
    high = value.astype(jnp.bfloat16)
    return high, (value - high.astype(jnp.float32)).astype(jnp.bfloat16)


def imaging(slots, occ_ref, spec_ref, targ_ref, kr_ref, ki_ref, h_ref, ht_ref, b_ref, g_ref, out_ref, p_ref, e_ref):
    wide = BATCH * 2 * BW

    def tile(item, carry):
        col, slot = item // slots, item % slots

        @pl.when(occ_ref[slot, col] == 0)
        def _():
            out_ref[col, pl.ds(pl.multiple_of(slot * FREQ, FREQ), FREQ), :] = jnp.zeros((FREQ, 2 * FREQ), jnp.float32)

        @pl.when(occ_ref[slot, col] != 0)
        def _():
            m = spec_ref[col, pl.ds(pl.multiple_of(slot * FREQ, FREQ), FREQ), :]
            mr, mi = m[:, :FREQ], m[:, FREQ:]
            first = jnp.concatenate([jnp.concatenate([mr, mi] * 2, 1), jnp.concatenate([-mi, mr] * 2, 1)], 0)
            second = jnp.concatenate([jnp.concatenate([-mi, mr] * 2, 1), jnp.concatenate([-mr, -mi] * 2, 1)], 0)
            left_half = lax.broadcasted_iota(jnp.int32, (2 * FREQ, 128), 1) < 2 * FREQ
            for base in range(0, KERNELS, BATCH):
                parts = []
                for k in range(base, base + BATCH):
                    prod = kr_ref[k] * first + ki_ref[k] * second
                    high = prod.astype(jnp.bfloat16).astype(jnp.float32)
                    parts.append(jnp.where(left_half, prod, prod - high).astype(jnp.bfloat16))
                half = mixed_dot(jnp.concatenate(parts, 0), b_ref[0]).astype(jnp.bfloat16)
                p_ref[base * 2 * FREQ : (base + BATCH) * 2 * FREQ, :] = half
            intensity = jnp.zeros((BH, BW), jnp.float32)
            for base in range(0, KERNELS, BATCH):
                rhs = jnp.concatenate(
                    [p_ref[k * 2 * FREQ : (k + 1) * 2 * FREQ, :] for k in range(base, base + BATCH)], 1
                )
                field = mixed_dot(h_ref[0], rhs)
                e_ref[:, base * 2 * BW : base * 2 * BW + wide] = field
                square = field * field
                for lane in range(0, wide, BW):
                    intensity = intensity + square[:, lane : lane + BW]
            wanted = targ_ref[col, pl.ds(pl.multiple_of(slot * BH, BH), BH), :].astype(jnp.float32)
            resist = jax.nn.sigmoid(STEEP * (intensity - THRESHOLD))
            sens = (2.0 * 2.0 * STEEP) * (resist - wanted) * resist * (1.0 - resist)
            many = jnp.concatenate([sens] * (2 * BATCH), 1)
            sum_r = jnp.zeros((2 * FREQ, 128), jnp.float32)
            sum_i = jnp.zeros((2 * FREQ, 128), jnp.float32)
            for base in range(0, KERNELS, BATCH):
                cot = (e_ref[:, base * 2 * BW : base * 2 * BW + wide] * many).astype(jnp.bfloat16)
                pulled = mixed_dot(ht_ref[0], cot)
                high, low = two_parts(pulled)
                lhs = jnp.concatenate(
                    [
                        jnp.concatenate([high[:, at : at + 2 * BW], low[:, at : at + 2 * BW]], 1)
                        for at in range(0, wide, 2 * BW)
                    ],
                    0,
                )
                back = mixed_dot(lhs, g_ref[0])
                for n in range(BATCH):
                    z = back[n * 2 * FREQ : (n + 1) * 2 * FREQ]
                    sum_r = sum_r + kr_ref[base + n] * z
                    sum_i = sum_i + ki_ref[base + n] * z
            by_r = sum_r[:FREQ, : 2 * FREQ] + sum_r[FREQ:, 2 * FREQ :]
            by_i = sum_i[:FREQ, : 2 * FREQ] + sum_i[FREQ:, 2 * FREQ :]
            grad = jnp.concatenate(
                [by_r[:, :FREQ] + by_i[:, FREQ:], by_r[:, FREQ:] - by_i[:, :FREQ]], 1
            )
            out_ref[col, pl.ds(pl.multiple_of(slot * FREQ, FREQ), FREQ), :] = grad

        return carry

    lax.fori_loop(0, slots * GROUP, tile, 0)


def image(occ, spec, targ, kr, ki, place, slots):
    whole = lambda a: pl.BlockSpec(a.shape, lambda i, p, *_: (0,) * a.ndim)
    inv = jnp.asarray(INVERSE.reshape(2, BH, 2 * FREQ))
    inv_t = jnp.asarray(np.ascontiguousarray(INVERSE.reshape(2, BH, 2 * FREQ).transpose(0, 2, 1)))
    there, back = jnp.asarray(THERE), jnp.asarray(BACK)

    def body(place_ref, *refs):
        imaging(slots, *refs)

    return pl.pallas_call(
        body,
        grid_spec=pltpu.PrefetchScalarGridSpec(
            num_scalar_prefetch=1,
            grid=(1,),
            in_specs=[
                pl.BlockSpec(memory_space=pltpu.SMEM),
                whole(spec),
                whole(targ),
                whole(kr),
                whole(ki),
                pl.BlockSpec((1, BH, 2 * FREQ), lambda i, p: (p[0] % 2, 0, 0)),
                pl.BlockSpec((1, 2 * FREQ, BH), lambda i, p: (p[0] % 2, 0, 0)),
                pl.BlockSpec((1,) + THERE.shape[1:], lambda i, p: (p[0] // 2, 0, 0)),
                pl.BlockSpec((1,) + BACK.shape[1:], lambda i, p: (p[0] // 2, 0, 0)),
            ],
            out_specs=whole(spec),
            scratch_shapes=[
                pltpu.VMEM((KERNELS * 2 * FREQ, 2 * BW), jnp.bfloat16),
                pltpu.VMEM((BH, KERNELS * 2 * BW), jnp.float32),
            ],
        ),
        out_shape=jax.ShapeDtypeStruct(spec.shape, jnp.float32),
        compiler_params=pltpu.CompilerParams(vmem_limit_bytes=40 * 1024 * 1024),
    )(place, occ, spec, targ, kr, ki, inv, inv_t, there, back)


def shifted(value, axis, step):
    count = lax.axis_size(axis)
    return lax.ppermute(value, axis, [(i, i + step) for i in range(count) if 0 <= i + step < count])


def on_device(mask_field, target_field, occupancy, kernels, weights):
    height, width = mask_field.shape
    slots = height // TILE
    size = lax.axis_size("img")
    groups = [list(range(at, at + GROUP)) for at in range(0, size, GROUP)]
    band, column = lax.axis_index("own"), lax.axis_index("img")
    place = column % GROUP
    root = jnp.sqrt(weights)[:, None, None]
    dup = lambda part: jnp.tile(root * kernels[part], (1, 2, 4))
    kr, ki = dup(0), dup(1)
    occ = lax.dynamic_slice(occupancy, (band * slots, column - place), (slots, GROUP))
    targ = target_field.reshape(slots, 2, BH, TILE // BW, BW).transpose(3, 1, 0, 2, 4)
    targ = targ.reshape(GROUP, slots * BH, BW)
    targ = lax.all_to_all(targ, "img", 0, 0, axis_index_groups=groups)

    above = shifted(mask_field[height - AMBIT :], "own", 1)
    below = shifted(mask_field[:AMBIT], "own", -1)
    tall = jnp.concatenate([above, mask_field, below], 0)
    forward = jnp.asarray(FORWARD)
    upper = jnp.concatenate([mixed_dot(forward, tall[s * TILE : s * TILE + PAD]) for s in range(slots)], 0)
    upper = upper.astype(jnp.bfloat16)
    across = jnp.asarray(spread(1))
    three = mixed_dot(upper, across.T)
    spec = three[:, 64:128] + shifted(three[:, :64], "img", -1) + shifted(three[:, 128:], "img", 1)
    spec = spec.reshape(slots, 2, FREQ, 2, FREQ)
    spec = jnp.concatenate([spec[:, 0, :, 0] - spec[:, 1, :, 1], spec[:, 0, :, 1] + spec[:, 1, :, 0]], -1)
    spec = lax.all_gather(spec.reshape(slots * FREQ, 2 * FREQ), "img", axis_index_groups=groups)

    grad = image(occ, spec, targ, kr, ki, place.reshape(1).astype(jnp.int32), slots)
    grad = lax.all_to_all(grad, "img", 0, 0, axis_index_groups=groups).sum(0)
    three = jnp.concatenate([shifted(grad, "img", 1), grad, shifted(grad, "img", -1)], 1)
    three = three.reshape(slots, FREQ, 3, 2, FREQ)
    gr, gi = three[:, :, :, 0], three[:, :, :, 1]
    both = jnp.stack([jnp.stack([gr, gi], 3), jnp.stack([gi, -gr], 3)], 1)
    high, low = two_parts(both.reshape(slots * 2 * FREQ, 6 * FREQ))
    lowered = (mixed_dot(high, across) + mixed_dot(low, across)).astype(jnp.bfloat16)
    from_above = shifted(lowered[-2 * FREQ :], "own", 1)
    from_below = shifted(lowered[: 2 * FREQ], "own", -1)
    lowered = jnp.concatenate([from_above, lowered, from_below], 0)
    values = mask_field.astype(jnp.float32)
    penalty = GAMMA * 4.0 * values * (values * values - 1.0)
    return mixed_dot(jnp.asarray(np.ascontiguousarray(spread(slots).T)), lowered) + penalty


def solution(mesh):
    return jax.shard_map(
        on_device,
        mesh=mesh,
        in_specs=(P("own", "img"), P("own", "img"), P(), P(), P()),
        out_specs=P("own", "img"),
        check_vma=False,
    )
```

```python
import math

import jax
import jax.numpy as jnp
import numpy as np
from jax import lax
from jax.experimental import pallas as pl
from jax.experimental.pallas import tpu as pltpu
from jax.sharding import PartitionSpec as P

TILE = 512
AMBIT = 64
FREQ = 32
KERNELS = 24
PAD = 640
STEEP = 2.0
THRESHOLD = 1.5
GAMMA = 0.25
GROUP = 8
BH = 256
BW = 128
BATCH = 4


def tables():
    freqs = np.arange(FREQ) - FREQ // 2
    turn = np.float32(2.0 * math.pi / PAD)
    phase = ((freqs[:, None] * np.arange(PAD)[None, :]) % PAD).astype(np.float32) * turn
    back = (((np.arange(TILE) + AMBIT)[:, None] * freqs[None, :]) % PAD).astype(np.float32) * turn
    bf = lambda a: np.asarray(a, np.float32).astype(jnp.bfloat16)
    return (
        bf(np.cos(phase) / np.float32(math.sqrt(PAD))),
        bf(-np.sin(phase) / np.float32(math.sqrt(PAD))),
        bf(np.cos(back) / np.float32(math.sqrt(FREQ))),
        bf(np.sin(back) / np.float32(math.sqrt(FREQ))),
    )


FC, FS, HC, HS = tables()
FORWARD = np.concatenate([FC, FS], 0)
INVERSE = np.concatenate([HC, HS], 1)


def spread(count):
    length = count * TILE
    out = np.zeros((count + 2, 2 * FREQ, length), jnp.bfloat16)
    for tile in range(-1, count + 1):
        start = tile * TILE - AMBIT
        low, high = max(start, 0), min(start + PAD, length)
        out[tile + 1, :, low:high] = FORWARD[:, low - start : high - start]
    return out.reshape(-1, length)


def column_tables():
    there, back = [], []
    for block in range(TILE // BW):
        c = HC[block * BW : (block + 1) * BW].astype(np.float32)
        s = HS[block * BW : (block + 1) * BW].astype(np.float32)
        one = np.block([[c.T, s.T], [-s.T, c.T]])
        there.append(np.concatenate([one, one], 0))
        adj = np.concatenate([np.block([[c, -s], [s, c]]), np.block([[-s, -c], [c, -s]])], 1)
        back.append(np.concatenate([adj, adj], 0))
    return np.stack(there).astype(jnp.bfloat16), np.stack(back).astype(jnp.bfloat16)


THERE, BACK = column_tables()


def exchange_tables(slots):
    rows = spread(slots).reshape(slots + 2, 2, FREQ, -1)[1:-1].transpose(1, 0, 2, 3).reshape(2 * slots * FREQ, -1)
    edge = np.zeros((2, slots, FREQ, 2 * AMBIT), jnp.bfloat16)
    both = FORWARD.reshape(2, FREQ, PAD)
    edge[:, 0, :, :AMBIT] = both[:, :, :AMBIT]
    edge[:, -1, :, AMBIT:] = both[:, :, -AMBIT:]
    near = spread(1).reshape(3, 2, FREQ, TILE)
    cols = []
    for which in (1, 0, 2):
        c, s = near[which].astype(np.float32)
        cols += [np.block([[c.T, s.T], [-s.T, c.T]])] * 2
    return rows, edge.reshape(2 * slots * FREQ, -1), np.concatenate(cols, 1).astype(jnp.bfloat16)


def lowering_tables():
    near = spread(1).reshape(3, 2, FREQ, TILE).astype(np.float32)
    full = [np.block([[c, -s], [s, c]]) for c, s in near]
    cut = [np.block([[c, -s], [s, c]]) for c, s in (near[0][:, :, :128], near[2][:, :, -128:])]
    twice = lambda a: np.concatenate([a, a], 0).astype(jnp.bfloat16)
    return twice(full[1]), np.stack([twice(cut[0]), twice(cut[1])])


def mixed_dot(left, right):
    return jnp.dot(left, right, preferred_element_type=jnp.float32)


def two_parts(value):
    high = value.astype(jnp.bfloat16)
    return high, (value - high.astype(jnp.float32)).astype(jnp.bfloat16)


MESH = pl.DeviceIdType.MESH
NEAR = [(dy, dx) for dy in (-1, 0, 1) for dx in (-1, 0, 1) if (dy, dx) != (0, 0)]


class Place:
    def __init__(self, bands, size):
        self.bands, self.size = bands, size
        self.band, self.column = lax.axis_index("own"), lax.axis_index("img")
        self.index = lax.rem(self.column, GROUP)

    def peer(self, step):
        index = lax.rem(self.index + step, GROUP)
        return index, (self.band, self.column - self.index + index)

    def near(self, dy, dx):
        row, col = self.band + dy, self.column + dx
        there = (row >= 0) & (row < self.bands) & (col >= 0) & (col < self.size)
        return there, (row, col)

    def greet(self, offsets):
        barrier = pltpu.get_barrier_semaphore()
        count = jnp.int32(GROUP - 1)
        for step in range(1, GROUP):
            pl.semaphore_signal(barrier, inc=1, device_id=self.peer(step)[1], device_id_type=MESH)
        for offset in offsets:
            there, device = self.near(*offset)
            count = count + there.astype(jnp.int32)

            @pl.when(there)
            def _():
                pl.semaphore_signal(barrier, inc=1, device_id=device, device_id_type=MESH)

        pl.semaphore_wait(barrier, count)


def push(src, dst, send, recv, device):
    return pltpu.make_async_remote_copy(
        src_ref=src, dst_ref=dst, send_sem=send, recv_sem=recv, device_id=device, device_id_type=MESH
    )


def block_at(index):
    row = pl.multiple_of(lax.rem(index, 2) * BH, BH)
    col = pl.multiple_of(lax.div(index, 2) * BW, BW)
    return row, col


def exchange(
    bands, size, slots, mask_ref, targ_ref, rows_ref, edge_ref, cols_ref, spec_ref, held_ref,
    halo, out_msg, side, halo_send, halo_recv, side_send, side_recv, spec_send, spec_recv, targ_send, targ_recv, own_sem,
):
    at = Place(bands, size)
    height = slots * TILE
    at.greet([(-1, 0), (1, 0), (0, -1), (0, 1)])

    vertical = []
    for n, dy in enumerate((-1, 1)):
        there, device = at.near(dy, 0)
        src = mask_ref.at[pl.ds(0 if dy < 0 else height - AMBIT, AMBIT)]
        copy = push(src, halo.at[pl.ds((1 - n) * AMBIT, AMBIT)], halo_send.at[n], halo_recv.at[n], device)
        vertical.append((there, copy))
        pl.when(there)(copy.start)

    moves = []
    for step in range(1, GROUP):
        index, device = at.peer(step)
        row, col = block_at(index)
        for slot in range(slots):
            copy = push(
                targ_ref.at[pl.ds(slot * TILE + row, BH), pl.ds(col, BW)],
                held_ref.at[at.index, pl.ds(slot * BH, BH)],
                targ_send.at[step - 1, slot], targ_recv.at[step - 1, slot], device,
            )
            copy.start()
            moves.append(copy)
    row, col = block_at(at.index)
    for slot in range(slots):
        copy = pltpu.make_async_copy(
            targ_ref.at[pl.ds(slot * TILE + row, BH), pl.ds(col, BW)],
            held_ref.at[at.index, pl.ds(slot * BH, BH)],
            own_sem.at[slot],
        )
        copy.start()
        moves.append(copy)

    upper = mixed_dot(rows_ref[...], mask_ref[...])
    for n, (there, copy) in enumerate(vertical):
        source, _ = at.near(1 if n == 0 else -1, 0)
        pl.when(source)(copy.wait_recv)

        @pl.when(jnp.logical_not(source))
        def _():
            halo[(1 - n) * AMBIT : (2 - n) * AMBIT, :] = jnp.zeros((AMBIT, TILE), jnp.bfloat16)

    upper = (upper + mixed_dot(edge_ref[...], halo[...])).astype(jnp.bfloat16)
    half = slots * FREQ
    three = mixed_dot(jnp.concatenate([upper[:half], upper[half:]], 1), cols_ref[...])
    first = lax.broadcasted_iota(jnp.int32, (FREQ, 128), 1) < 2 * FREQ
    own, left, right = [jnp.where(first, three[:FREQ, a : a + 128], three[FREQ:, a : a + 128]) for a in (0, 128, 256)]
    out_msg[0] = left
    out_msg[1] = right
    sideways = []
    for n, dx in enumerate((-1, 1)):
        there, device = at.near(0, dx)
        copy = push(out_msg.at[n], side.at[n], side_send.at[n], side_recv.at[n], device)
        sideways.append((there, copy))
        pl.when(there)(copy.start)
    for n, (there, copy) in enumerate(sideways):
        source, _ = at.near(0, 1 if n == 0 else -1)
        pl.when(source)(copy.wait_recv)

        @pl.when(jnp.logical_not(source))
        def _():
            side[n] = jnp.zeros((FREQ, 128), jnp.float32)

    spec_ref[at.index] = own + side[0] + side[1]
    for step in range(1, GROUP):
        _, device = at.peer(step)
        copy = push(
            spec_ref.at[at.index], spec_ref.at[at.index], spec_send.at[step - 1], spec_recv.at[step - 1], device
        )
        copy.start()
        moves.append(copy)
    for there, copy in vertical + sideways:
        pl.when(there)(copy.wait_send)
    for copy in moves:
        copy.wait()


VMEM = pl.BlockSpec(memory_space=pltpu.VMEM)


def exchange_call(mask_field, target_field, bands, size, slots):
    rows, edge, cols = [jnp.asarray(a) for a in exchange_tables(slots)]
    dma = pltpu.SemaphoreType.DMA
    return pl.pallas_call(
        lambda *refs: exchange(bands, size, slots, *refs),
        out_shape=[
            jax.ShapeDtypeStruct((GROUP, FREQ, 128), jnp.float32),
            jax.ShapeDtypeStruct((GROUP, slots * BH, BW), jnp.bfloat16),
        ],
        in_specs=[VMEM, pl.BlockSpec(memory_space=pl.ANY), VMEM, VMEM, VMEM],
        out_specs=[VMEM, VMEM],
        scratch_shapes=[
            pltpu.VMEM((2 * AMBIT, TILE), jnp.bfloat16),
            pltpu.VMEM((2, FREQ, 128), jnp.float32),
            pltpu.VMEM((2, FREQ, 128), jnp.float32),
            dma((2,)), dma((2,)), dma((2,)), dma((2,)),
            dma((GROUP - 1,)), dma((GROUP - 1,)),
            dma((GROUP - 1, slots)), dma((GROUP - 1, slots)), dma((slots,)),
        ],
        compiler_params=pltpu.CompilerParams(
            collective_id=0, has_side_effects=True, vmem_limit_bytes=32 * 1024 * 1024
        ),
    )(mask_field, target_field, rows, edge, cols)


def gathering(
    bands, size, grad_ref, own_ref, beside_ref, low_ref,
    part, full, near, part_send, part_recv, near_send, near_recv,
):
    at = Place(bands, size)
    at.greet(NEAR)
    moves = []
    for step in range(1, GROUP):
        index, device = at.peer(step)
        copy = push(grad_ref.at[index], part.at[step - 1], part_send.at[step - 1], part_recv.at[step - 1], device)
        copy.start()
        moves.append(copy)
    total = grad_ref[at.index]
    for n, copy in enumerate(moves):
        copy.wait_recv()
        total = total + part[n]
    full[...] = total
    sent = []
    for n, offset in enumerate(NEAR):
        there, device = at.near(*offset)
        copy = push(full, near.at[n], near_send.at[n], near_recv.at[n], device)
        sent.append((there, copy))
        pl.when(there)(copy.start)
    for n, (dy, dx) in enumerate(NEAR):
        source, _ = at.near(-dy, -dx)
        pl.when(source)(sent[n][1].wait_recv)

        @pl.when(jnp.logical_not(source))
        def _():
            near[n] = jnp.zeros((FREQ, 128), jnp.float32)

    first = lax.broadcasted_iota(jnp.int32, (FREQ, 128), 1) < 2 * FREQ

    def column(dx):
        get = lambda dy: total if (dy, dx) == (0, 0) else near[NEAR.index((-dy, -dx))]
        upper, middle, lower = get(-1), get(0), get(1)
        return two_parts(
            jnp.concatenate(
                [
                    jnp.where(first, 0.0, upper),
                    jnp.where(first, middle, 0.0),
                    jnp.where(first, 0.0, middle),
                    jnp.where(first, lower, 0.0),
                ],
                0,
            )
        )

    def product(dx, table):
        high, low = column(dx)
        return mixed_dot(high, table) + mixed_dot(low, table)

    own = product(0, own_ref[...])
    left = product(-1, beside_ref[0])
    right = product(1, beside_ref[1])
    for part_no in range(2):
        base = part_no * TILE
        value = own[:, base : base + TILE]
        value = jnp.concatenate(
            [
                value[:, :128] + left[:, part_no * 128 : part_no * 128 + 128],
                value[:, 128:-128],
                value[:, -128:] + right[:, part_no * 128 : part_no * 128 + 128],
            ],
            1,
        ).astype(jnp.bfloat16)
        for tile in range(4):
            low_ref[(2 * tile + part_no) * FREQ : (2 * tile + part_no + 1) * FREQ, :] = value[
                tile * FREQ : (tile + 1) * FREQ
            ]
    for copy in moves:
        copy.wait_send()
    for there, copy in sent:
        pl.when(there)(copy.wait_send)


def gathering_call(grad, bands, size):
    own, beside = [jnp.asarray(a) for a in lowering_tables()]
    dma = pltpu.SemaphoreType.DMA
    return pl.pallas_call(
        lambda *refs: gathering(bands, size, *refs),
        out_shape=jax.ShapeDtypeStruct((8 * FREQ, TILE), jnp.bfloat16),
        in_specs=[VMEM, VMEM, VMEM],
        out_specs=VMEM,
        scratch_shapes=[
            pltpu.VMEM((GROUP - 1, FREQ, 128), jnp.float32),
            pltpu.VMEM((FREQ, 128), jnp.float32),
            pltpu.VMEM((len(NEAR), FREQ, 128), jnp.float32),
            dma((GROUP - 1,)), dma((GROUP - 1,)), dma((len(NEAR),)), dma((len(NEAR),)),
        ],
        compiler_params=pltpu.CompilerParams(
            collective_id=1, has_side_effects=True, vmem_limit_bytes=32 * 1024 * 1024
        ),
    )(grad, own, beside)


def finish_call(lowered, mask_field, slots):
    table = jnp.asarray(np.ascontiguousarray(spread(slots).T))
    height, width = mask_field.shape

    def finish(table_ref, low_ref, mask_ref, out_ref):
        values = mask_ref[...].astype(jnp.float32)
        penalty = GAMMA * 4.0 * values * (values * values - 1.0)
        out_ref[...] = mixed_dot(table_ref[...], low_ref[...]) + penalty

    rows = 256
    return pl.pallas_call(
        finish,
        grid=(height // rows,),
        out_shape=jax.ShapeDtypeStruct((height, width), jnp.float32),
        in_specs=[
            pl.BlockSpec((rows, table.shape[1]), lambda i: (i, 0)),
            pl.BlockSpec(lowered.shape, lambda i: (0, 0)),
            pl.BlockSpec((rows, width), lambda i: (i, 0)),
        ],
        out_specs=pl.BlockSpec((rows, width), lambda i: (i, 0)),
    )(table, lowered, mask_field)


def imaging(slots, root_ref, occ_ref, spec_ref, targ_ref, kern_ref, h_ref, ht_ref, b_ref, g_ref, out_ref, kr_ref, ki_ref, p_ref, e_ref):
    wide = BATCH * 2 * BW
    for k in range(KERNELS):
        for part, ref in ((0, kr_ref), (1, ki_ref)):
            ref[k] = jnp.concatenate([kern_ref[part, k]] * 4, 1) * root_ref[k]
    out_ref[...] = jnp.zeros(out_ref.shape, jnp.float32)
    lane = lax.broadcasted_iota(jnp.int32, (FREQ, 128), 1)
    low_half = lane < 2 * FREQ
    sign = jnp.where(lane % (2 * FREQ) < FREQ, -1.0, 1.0)

    def tile(item, carry):
        col, slot = item // slots, item % slots

        @pl.when(occ_ref[slot, col] != 0)
        def _():
            packed = spec_ref[col]
            here = (lane // (2 * FREQ)) == slot
            m = jnp.where(here, packed, pltpu.roll(packed, 64, 1))
            n = sign * pltpu.roll(m, 32, 1)
            for base in range(0, KERNELS, BATCH):
                parts = []
                for k in range(base, base + BATCH):
                    kr, ki = kr_ref[k], ki_ref[k]
                    for prod in (kr * m + ki * n, kr * n - ki * m):
                        high = prod.astype(jnp.bfloat16).astype(jnp.float32)
                        parts.append(jnp.where(low_half, prod, prod - high).astype(jnp.bfloat16))
                half = mixed_dot(jnp.concatenate(parts, 0), b_ref[0]).astype(jnp.bfloat16)
                p_ref[base * 2 * FREQ : (base + BATCH) * 2 * FREQ, :] = half
            intensity = jnp.zeros((BH, BW), jnp.float32)
            for base in range(0, KERNELS, BATCH):
                rhs = jnp.concatenate(
                    [p_ref[k * 2 * FREQ : (k + 1) * 2 * FREQ, :] for k in range(base, base + BATCH)], 1
                )
                field = mixed_dot(h_ref[0], rhs)
                e_ref[:, base * 2 * BW : base * 2 * BW + wide] = field
                square = field * field
                for start in range(0, wide, BW):
                    intensity = intensity + square[:, start : start + BW]
            wanted = targ_ref[col, pl.ds(pl.multiple_of(slot * BH, BH), BH), :].astype(jnp.float32)
            resist = jax.nn.sigmoid(STEEP * (intensity - THRESHOLD))
            sens = (2.0 * 2.0 * STEEP) * (resist - wanted) * resist * (1.0 - resist)
            many = jnp.concatenate([sens] * (2 * BATCH), 1)
            sums = [jnp.zeros((FREQ, 128), jnp.float32) for _ in range(4)]
            for base in range(0, KERNELS, BATCH):
                cot = (e_ref[:, base * 2 * BW : base * 2 * BW + wide] * many).astype(jnp.bfloat16)
                pulled = mixed_dot(ht_ref[0], cot)
                high, low = two_parts(pulled)
                lhs = jnp.concatenate(
                    [
                        jnp.concatenate([high[:, at : at + 2 * BW], low[:, at : at + 2 * BW]], 1)
                        for at in range(0, wide, 2 * BW)
                    ],
                    0,
                )
                back = mixed_dot(lhs, g_ref[0])
                for n_k in range(BATCH):
                    z = back[n_k * 2 * FREQ : (n_k + 1) * 2 * FREQ]
                    kr, ki = kr_ref[base + n_k], ki_ref[base + n_k]
                    sums = [
                        sums[0] + kr * z[:FREQ], sums[1] + kr * z[FREQ:],
                        sums[2] + ki * z[:FREQ], sums[3] + ki * z[FREQ:],
                    ]
            by_r = sums[0] + pltpu.roll(sums[1], 64, 1)
            by_i = sums[2] + pltpu.roll(sums[3], 64, 1)
            grad = by_r + jnp.where(lane < FREQ, pltpu.roll(by_i, 96, 1), -pltpu.roll(by_i, 32, 1))
            grad = jnp.where(low_half, grad, pltpu.roll(grad, 64, 1))
            out_ref[col] = jnp.where(here, grad, out_ref[col])

        return carry

    lax.fori_loop(0, slots * GROUP, tile, 0)


def image_call(place, root, occ, spec, targ, kernels, slots):
    whole = lambda a: pl.BlockSpec(a.shape, lambda i, p, *_: (0,) * a.ndim)
    inv = jnp.asarray(INVERSE.reshape(2, BH, 2 * FREQ))
    inv_t = jnp.asarray(np.ascontiguousarray(INVERSE.reshape(2, BH, 2 * FREQ).transpose(0, 2, 1)))
    there, back = jnp.asarray(THERE), jnp.asarray(BACK)

    def body(place_ref, *refs):
        imaging(slots, *refs)

    return pl.pallas_call(
        body,
        grid_spec=pltpu.PrefetchScalarGridSpec(
            num_scalar_prefetch=1,
            grid=(1,),
            in_specs=[
                pl.BlockSpec(memory_space=pltpu.SMEM),
                pl.BlockSpec(memory_space=pltpu.SMEM),
                whole(spec),
                whole(targ),
                whole(kernels),
                pl.BlockSpec((1, BH, 2 * FREQ), lambda i, p: (p[0] % 2, 0, 0)),
                pl.BlockSpec((1, 2 * FREQ, BH), lambda i, p: (p[0] % 2, 0, 0)),
                pl.BlockSpec((1,) + THERE.shape[1:], lambda i, p: (p[0] // 2, 0, 0)),
                pl.BlockSpec((1,) + BACK.shape[1:], lambda i, p: (p[0] // 2, 0, 0)),
            ],
            out_specs=whole(spec),
            scratch_shapes=[
                pltpu.VMEM((KERNELS, FREQ, 128), jnp.float32),
                pltpu.VMEM((KERNELS, FREQ, 128), jnp.float32),
                pltpu.VMEM((KERNELS * 2 * FREQ, 2 * BW), jnp.bfloat16),
                pltpu.VMEM((BH, KERNELS * 2 * BW), jnp.float32),
            ],
        ),
        out_shape=jax.ShapeDtypeStruct(spec.shape, jnp.float32),
        compiler_params=pltpu.CompilerParams(vmem_limit_bytes=40 * 1024 * 1024),
    )(place, root, occ, spec, targ, kernels, inv, inv_t, there, back)


def on_device(mask_field, target_field, occupancy, kernels, weights):
    slots = mask_field.shape[0] // TILE
    bands, size = lax.axis_size("own"), lax.axis_size("img")
    assert slots == 2 and size % GROUP == 0
    band, column = lax.axis_index("own"), lax.axis_index("img")
    place = column % GROUP
    occ = lax.dynamic_slice(occupancy, (band * slots, column - place), (slots, GROUP))
    spec, targ = exchange_call(mask_field, target_field, bands, size, slots)
    grad = image_call(
        place.reshape(1).astype(jnp.int32), jnp.sqrt(weights), occ, spec, targ, kernels, slots
    )
    lowered = gathering_call(grad, bands, size)
    return finish_call(lowered, mask_field, slots)


def solution(mesh):
    return jax.shard_map(
        on_device,
        mesh=mesh,
        in_specs=(P("own", "img"), P("own", "img"), P(), P(), P()),
        out_specs=P("own", "img"),
        check_vma=False,
    )
```

```python
import math

import jax
import jax.numpy as jnp
import numpy as np
from jax import lax
from jax.experimental import pallas as pl
from jax.experimental.pallas import tpu as pltpu
from jax.sharding import PartitionSpec as P

TILE = 512
AMBIT = 64
FREQ = 32
KERNELS = 24
PAD = 640
STEEP = 2.0
THRESHOLD = 1.5
GAMMA = 0.25
GRID = 64


def tables():
    freqs = np.arange(FREQ) - FREQ // 2
    turn = np.float32(2.0 * math.pi / PAD)
    phase = ((freqs[:, None] * np.arange(PAD)[None, :]) % PAD).astype(np.float32) * turn
    bf = lambda a: np.asarray(a, np.float32).astype(jnp.bfloat16)
    return (
        bf(np.cos(phase) / np.float32(math.sqrt(PAD))),
        bf(-np.sin(phase) / np.float32(math.sqrt(PAD))),
    )


FC, FS = tables()
FORWARD = np.concatenate([FC, FS], 0)


def spread(count):
    length = count * TILE
    out = np.zeros((count + 2, 2 * FREQ, length), jnp.bfloat16)
    for tile in range(-1, count + 1):
        start = tile * TILE - AMBIT
        low, high = max(start, 0), min(start + PAD, length)
        out[tile + 1, :, low:high] = FORWARD[:, low - start : high - start]
    return out.reshape(-1, length)


def two_tables(table):
    high = np.asarray(table).astype(jnp.bfloat16)
    return high, (table - high.astype(np.float64)).astype(jnp.bfloat16)


def grid_tables():
    freqs = np.arange(FREQ) - FREQ // 2
    turn = 2.0 * math.pi * (np.arange(GRID)[:, None] * freqs[None, :]) / GRID
    c, s = np.cos(turn) / math.sqrt(FREQ), np.sin(turn) / math.sqrt(FREQ)
    zero = np.zeros((2 * FREQ, 2 * GRID))
    one = np.block([[c.T, s.T], [-s.T, c.T]])
    there_high, there_low = two_tables(np.block([[one, zero], [zero, one]]))
    there = np.concatenate([there_high, there_high, there_low], 0)
    high, low = two_tables(np.concatenate([c, s], 1))
    rows = np.concatenate([high, high, low], 1)
    rows_back = np.concatenate([high.T, high.T, low.T], 1)
    zero = np.zeros((2 * GRID, 2 * FREQ))
    parts = []
    for adj in (np.block([[c, -s], [s, c]]), np.block([[-s, -c], [c, -s]])):
        parts.append(np.block([[adj, zero], [zero, adj]]))
    high, low = two_tables(np.concatenate(parts, 0))
    back = np.concatenate([high, high, low], 0)
    waves = np.arange(-(FREQ - 1), FREQ)
    apart = (np.arange(TILE) + AMBIT)[:, None] / PAD - np.arange(GRID)[None, :] / GRID
    fine = np.cos(2.0 * math.pi * apart[:, :, None] * waves).sum(-1) / GRID
    high, low = two_tables(fine)
    up = np.concatenate([high, high, low, np.zeros_like(low)], 1)
    down = np.concatenate([high.T, low.T], 0)
    down_cols = np.concatenate([high, high, low, low], 1)
    return there, rows, rows_back, back, up, np.ascontiguousarray(up.T), down, down_cols


def exchange_tables(slots):
    rows = spread(slots).reshape(slots + 2, 2, FREQ, -1)[1:-1].transpose(1, 0, 2, 3).reshape(2 * slots * FREQ, -1)
    edge = np.zeros((2, slots, FREQ, 2 * AMBIT), jnp.bfloat16)
    both = FORWARD.reshape(2, FREQ, PAD)
    edge[:, 0, :, :AMBIT] = both[:, :, :AMBIT]
    edge[:, -1, :, AMBIT:] = both[:, :, -AMBIT:]
    near = spread(1).reshape(3, 2, FREQ, TILE)
    cols = []
    for which in (1, 1, 0, 2):
        c, s = near[which].astype(np.float32)
        cols.append(np.block([[c.T, s.T], [-s.T, c.T]]))
    return rows, edge.reshape(2 * slots * FREQ, -1), np.concatenate(cols, 1).astype(jnp.bfloat16)


def lowering_tables():
    near = spread(1).reshape(3, 2, FREQ, TILE).astype(np.float32)
    full = [np.block([[c, -s], [s, c]]) for c, s in near]
    cut = [np.block([[c, -s], [s, c]]) for c, s in (near[0][:, :, :128], near[2][:, :, -128:])]
    twice = lambda a: np.concatenate([a, a], 0).astype(jnp.bfloat16)
    return twice(full[1]), np.stack([twice(cut[0]), twice(cut[1])])


def mixed_dot(left, right):
    return jnp.dot(left, right, preferred_element_type=jnp.float32)


def two_parts(value):
    high = value.astype(jnp.bfloat16)
    return high, (value - high.astype(jnp.float32)).astype(jnp.bfloat16)


MESH = pl.DeviceIdType.MESH
VMEM = pl.BlockSpec(memory_space=pltpu.VMEM)
NEAR = [(dy, dx) for dy in (-1, 0, 1) for dx in (-1, 0, 1) if (dy, dx) != (0, 0)]


class Place:
    def __init__(self, bands, size):
        self.bands, self.size = bands, size
        self.band, self.column = lax.axis_index("own"), lax.axis_index("img")

    def near(self, dy, dx):
        row, col = self.band + dy, self.column + dx
        there = (row >= 0) & (row < self.bands) & (col >= 0) & (col < self.size)
        return there, (row, col)

    def greet(self, offsets):
        barrier = pltpu.get_barrier_semaphore()
        count = jnp.int32(0)
        for offset in offsets:
            there, device = self.near(*offset)
            count = count + there.astype(jnp.int32)

            @pl.when(there)
            def _():
                pl.semaphore_signal(barrier, inc=1, device_id=device, device_id_type=MESH)

        pl.semaphore_wait(barrier, count)


def push(src, dst, send, recv, device):
    return pltpu.make_async_remote_copy(
        src_ref=src, dst_ref=dst, send_sem=send, recv_sem=recv, device_id=device, device_id_type=MESH
    )


def swapped(value, lane):
    return jnp.where(lane % 64 < 32, pltpu.roll(value, 96, 1), pltpu.roll(value, 32, 1))


def spectrum_gradients(m, flags, wanted, kern_ref, root_ref, t, sens_ref):
    lane = lax.broadcasted_iota(jnp.int32, (FREQ, 128), 1)
    sign = jnp.where(lane % 64 < 32, -1.0, 1.0)
    n = sign * swapped(m, lane)
    spectra, parts = [], []
    for k in range(KERNELS):
        kr, ki = [jnp.concatenate([kern_ref[part, k]] * 4, 1) * root_ref[k] for part in (0, 1)]
        spectra.append((kr, ki))
        parts += [kr * m + ki * n, kr * n - ki * m]
    high, low = two_parts(jnp.concatenate(parts, 0))
    half = mixed_dot(jnp.concatenate([high, low, high], 1), t["there"][...])
    high, low = two_parts(half)
    fields = []
    total = jnp.zeros((GRID, 256), jnp.float32)
    for k in range(KERNELS):
        at = slice(k * 64, (k + 1) * 64)
        field = mixed_dot(t["rows"][...], jnp.concatenate([high[at], low[at], high[at]], 0))
        fields.append(field)
        total = total + field * field
    coarse = jnp.concatenate([total[:, :128], total[:, 128:]], 0)
    coarse = coarse + pltpu.roll(coarse, 64, 1)
    high, low = two_parts(coarse)
    first = lax.broadcasted_iota(jnp.int32, (2 * GRID, 128), 1) < 64
    zero = jnp.zeros((2 * GRID, 128), jnp.float32)
    high32, low32 = high.astype(jnp.float32), low.astype(jnp.float32)
    lhs = jnp.concatenate([jnp.where(first, high32, low32), jnp.where(first, high32, zero)], 1).astype(jnp.bfloat16)
    across = mixed_dot(lhs, t["up_t"][...])
    high, low = two_parts(across)
    rows = 128
    for slot in range(2):
        at = slice(slot * GRID, (slot + 1) * GRID)
        rhs = jnp.concatenate([high[at], low[at], high[at], jnp.zeros((GRID, TILE), jnp.bfloat16)], 0)
        for start in range(0, TILE, rows):
            intensity = mixed_dot(t["up"][start : start + rows, :], rhs)
            bend = jnp.tanh((0.5 * STEEP) * (intensity - THRESHOLD))
            goal = wanted[slot * TILE + start : slot * TILE + start + rows, :].astype(jnp.float32)
            sens = (0.5 * STEEP) * (1.0 + bend - 2.0 * goal) * (1.0 - bend * bend)
            sens_ref[start : start + rows, slot * TILE : (slot + 1) * TILE] = sens.astype(jnp.bfloat16)
    folded = mixed_dot(t["down"][...], sens_ref[...])
    folded = folded[:GRID] + folded[GRID:]
    high, low = two_parts(jnp.concatenate([folded[:, :TILE], folded[:, TILE:]], 0))
    grid = mixed_dot(jnp.concatenate([high, low], 0), t["down_cols"][...])
    grid = grid[:128, :128] + grid[:128, 128:] + grid[128:, :128]
    weight = jnp.concatenate([grid[:GRID], grid[GRID:]], 1)
    tops, bottoms = [], []
    for k in range(KERNELS):
        high, low = two_parts(fields[k] * weight)
        pulled = mixed_dot(t["rows_back"][...], jnp.concatenate([high, low, high], 0))
        tops.append(pulled[:FREQ])
        bottoms.append(pulled[FREQ:])
    high, low = two_parts(jnp.concatenate([jnp.concatenate(tops, 0), jnp.concatenate(bottoms, 0)], 1))
    back = mixed_dot(jnp.concatenate([high, low, high], 1), t["back"][...])
    sum_r = jnp.zeros((FREQ, 128), jnp.float32)
    sum_i = jnp.zeros((FREQ, 128), jnp.float32)
    for k in range(KERNELS):
        z = back[k * FREQ : (k + 1) * FREQ]
        sum_r = sum_r + spectra[k][0] * z
        sum_i = sum_i + spectra[k][1] * z
    grad = sum_r - sign * swapped(sum_i, lane)
    return jnp.where(jnp.where(lane < 64, flags[0], flags[1]) > 0, grad, 0.0)


NAMES = ["there", "rows", "rows_back", "back", "up", "up_t", "down", "down_cols"]
COPIED = ["mask", "row_table", "edge", "cols", "there", "rows", "up_t", "up", "target", "down", "down_cols", "rows_back", "back", "own", "beside"]


def whole(bands, size, slots, shapes, root_ref, occ_ref, kern_ref, *refs):
    count = len(COPIED)
    sources = dict(zip(COPIED, refs[:count]))
    low_ref = refs[count]
    held = dict(zip(COPIED, refs[count + 1 : 2 * count + 1]))
    (sens_ref, halo, out_msg, side, full, near, copy_sem,
     halo_send, halo_recv, side_send, side_recv, near_send, near_recv) = refs[2 * count + 1 :]
    at = Place(bands, size)
    height = slots * TILE
    copies = {}
    for n, name in enumerate(COPIED):
        copies[name] = pltpu.make_async_copy(sources[name], held[name], copy_sem.at[n])
        copies[name].start()
    at.greet(NEAR)

    vertical = []
    for n, dy in enumerate((-1, 1)):
        there, device = at.near(dy, 0)
        src = sources["mask"].at[pl.ds(0 if dy < 0 else height - AMBIT, AMBIT)]
        copy = push(src, halo.at[pl.ds((1 - n) * AMBIT, AMBIT)], halo_send.at[n], halo_recv.at[n], device)
        vertical.append((there, copy))
        pl.when(there)(copy.start)
    for name in ("mask", "row_table", "edge", "cols"):
        copies[name].wait()
    upper = mixed_dot(held["row_table"][...], held["mask"][...])
    for n, (there, copy) in enumerate(vertical):
        source, _ = at.near(1 if n == 0 else -1, 0)
        pl.when(source)(copy.wait_recv)

        @pl.when(jnp.logical_not(source))
        def _():
            halo[(1 - n) * AMBIT : (2 - n) * AMBIT, :] = jnp.zeros((AMBIT, TILE), jnp.bfloat16)

    upper = (upper + mixed_dot(held["edge"][...], halo[...])).astype(jnp.bfloat16)
    half = slots * FREQ
    three = mixed_dot(jnp.concatenate([upper[:half], upper[half:]], 1), held["cols"][...])
    first = lax.broadcasted_iota(jnp.int32, (FREQ, 128), 1) < 64
    own = jnp.where(first, three[:FREQ, :128], three[FREQ:, :128])
    out_msg[0] = jnp.where(first, three[:FREQ, 128:], pltpu.roll(three[FREQ:, 128:], 64, 1))
    out_msg[1] = jnp.where(first, pltpu.roll(three[:FREQ, 128:], 64, 1), three[FREQ:, 128:])
    sideways = []
    for n, dx in enumerate((-1, 1)):
        there, device = at.near(0, dx)
        copy = push(out_msg.at[n], side.at[n], side_send.at[n], side_recv.at[n], device)
        sideways.append((there, copy))
        pl.when(there)(copy.start)
    for n, (there, copy) in enumerate(sideways):
        source, _ = at.near(0, 1 if n == 0 else -1)
        pl.when(source)(copy.wait_recv)

        @pl.when(jnp.logical_not(source))
        def _():
            side[n] = jnp.zeros((FREQ, 128), jnp.float32)

    for name in COPIED[4:]:
        copies[name].wait()
    flags = [occ_ref[slot] for slot in range(slots)]
    total = spectrum_gradients(
        own + side[0] + side[1], flags, held["target"], kern_ref, root_ref, {n: held[n] for n in NAMES}, sens_ref
    )
    full[...] = total
    sent = []
    for n, offset in enumerate(NEAR):
        there, device = at.near(*offset)
        copy = push(full, near.at[n], near_send.at[n], near_recv.at[n], device)
        sent.append((there, copy))
        pl.when(there)(copy.start)
    for n, (dy, dx) in enumerate(NEAR):
        source, _ = at.near(-dy, -dx)
        pl.when(source)(sent[n][1].wait_recv)

        @pl.when(jnp.logical_not(source))
        def _():
            near[n] = jnp.zeros((FREQ, 128), jnp.float32)

    def product(dx, table):
        get = lambda dy: total if (dy, dx) == (0, 0) else near[NEAR.index((-dy, -dx))]
        upper, middle, lower = get(-1), get(0), get(1)
        stack = [
            jnp.where(first, 0.0, upper), jnp.where(first, middle, 0.0),
            jnp.where(first, 0.0, middle), jnp.where(first, lower, 0.0),
        ]
        high, low = two_parts(jnp.concatenate(stack, 0))
        return mixed_dot(high, table) + mixed_dot(low, table)

    own = product(0, held["own"][...])
    left = product(-1, held["beside"][0])
    right = product(1, held["beside"][1])
    for part in range(2):
        value = own[:, part * TILE : (part + 1) * TILE]
        span = slice(part * 128, part * 128 + 128)
        value = jnp.concatenate(
            [value[:, :128] + left[:, span], value[:, 128:-128], value[:, -128:] + right[:, span]], 1
        ).astype(jnp.bfloat16)
        for tile in range(slots + 2):
            low_ref[(2 * tile + part) * FREQ : (2 * tile + part + 1) * FREQ, :] = value[
                tile * FREQ : (tile + 1) * FREQ
            ]
    for there, copy in vertical + sideways + sent:
        pl.when(there)(copy.wait_send)


def whole_call(mask_field, target_field, occ, kernels, root, bands, size, slots):
    arrays = dict(zip(NAMES, grid_tables()))
    arrays["row_table"], arrays["edge"], arrays["cols"] = exchange_tables(slots)
    arrays["own"], arrays["beside"] = lowering_tables()
    arrays = {name: jnp.asarray(a) for name, a in arrays.items()}
    arrays["mask"], arrays["target"] = mask_field, target_field
    given = [arrays[name] for name in COPIED]
    dma = pltpu.SemaphoreType.DMA
    smem, hbm = pl.BlockSpec(memory_space=pltpu.SMEM), pl.BlockSpec(memory_space=pl.ANY)
    return pl.pallas_call(
        lambda *refs: whole(bands, size, slots, None, *refs),
        out_shape=jax.ShapeDtypeStruct(((slots + 2) * 2 * FREQ, TILE), jnp.bfloat16),
        in_specs=[smem, smem, VMEM] + [hbm] * len(given),
        out_specs=VMEM,
        scratch_shapes=[pltpu.VMEM(a.shape, a.dtype) for a in given]
        + [
            pltpu.VMEM((TILE, slots * TILE), jnp.bfloat16),
            pltpu.VMEM((2 * AMBIT, TILE), jnp.bfloat16),
            pltpu.VMEM((2, FREQ, 128), jnp.float32),
            pltpu.VMEM((2, FREQ, 128), jnp.float32),
            pltpu.VMEM((FREQ, 128), jnp.float32),
            pltpu.VMEM((len(NEAR), FREQ, 128), jnp.float32),
            dma((len(given),)),
            dma((2,)), dma((2,)), dma((2,)), dma((2,)), dma((len(NEAR),)), dma((len(NEAR),)),
        ],
        compiler_params=pltpu.CompilerParams(
            collective_id=0, has_side_effects=True, vmem_limit_bytes=52 * 1024 * 1024
        ),
    )(root, occ, kernels, *given)


def finish_call(lowered, mask_field, slots):
    table = jnp.asarray(np.ascontiguousarray(spread(slots).T))
    height, width = mask_field.shape
    rows = 128
    steps = height // rows

    def finish(table_ref, low_ref, mask_ref, out_ref, held, sems):
        copies = []
        for step in range(steps):
            span = pl.ds(step * rows, rows)
            values = mask_ref[span, :].astype(jnp.float32)
            penalty = GAMMA * 4.0 * values * (values * values - 1.0)
            held[span, :] = mixed_dot(table_ref[span, :], low_ref[...]) + penalty
            copies.append(pltpu.make_async_copy(held.at[span], out_ref.at[span], sems.at[step]))
            copies[-1].start()
        for copy in copies:
            copy.wait()

    return pl.pallas_call(
        finish,
        out_shape=jax.ShapeDtypeStruct((height, width), jnp.float32),
        in_specs=[VMEM, VMEM, VMEM],
        out_specs=pl.BlockSpec(memory_space=pl.ANY),
        scratch_shapes=[pltpu.VMEM((height, width), jnp.float32), pltpu.SemaphoreType.DMA((steps,))],
        compiler_params=pltpu.CompilerParams(vmem_limit_bytes=16 * 1024 * 1024),
    )(table, lowered, mask_field)


def on_device(mask_field, target_field, occupancy, kernels, weights):
    slots = mask_field.shape[0] // TILE
    bands, size = lax.axis_size("own"), lax.axis_size("img")
    assert slots == 2
    band, column = lax.axis_index("own"), lax.axis_index("img")
    occ = lax.dynamic_slice(occupancy, (band * slots, column), (slots, 1))[:, 0]
    lowered = whole_call(mask_field, target_field, occ, kernels, jnp.sqrt(weights), bands, size, slots)
    return finish_call(lowered, mask_field, slots)


def solution(mesh):
    return jax.shard_map(
        on_device,
        mesh=mesh,
        in_specs=(P("own", "img"), P("own", "img"), P(), P(), P()),
        out_specs=P("own", "img"),
        check_vma=False,
    )
```

```python
import math

import jax
import jax.numpy as jnp
import numpy as np
from jax import lax
from jax.experimental import pallas as pl
from jax.experimental.pallas import tpu as pltpu
from jax.sharding import PartitionSpec as P

TILE = 512
AMBIT = 64
FREQ = 32
KERNELS = 24
PAD = 640
STEEP = 2.0
THRESHOLD = 1.5
GAMMA = 0.25
VMEM_GRANT = 61 * 1024 * 1024
GRID = 64


def tables():
    freqs = np.arange(FREQ) - FREQ // 2
    turn = np.float32(2.0 * math.pi / PAD)
    phase = ((freqs[:, None] * np.arange(PAD)[None, :]) % PAD).astype(np.float32) * turn
    bf = lambda a: np.asarray(a, np.float32).astype(jnp.bfloat16)
    return (
        bf(np.cos(phase) / np.float32(math.sqrt(PAD))),
        bf(-np.sin(phase) / np.float32(math.sqrt(PAD))),
    )


FC, FS = tables()
FORWARD = np.concatenate([FC, FS], 0)


def spread(count):
    length = count * TILE
    out = np.zeros((count + 2, 2 * FREQ, length), jnp.bfloat16)
    for tile in range(-1, count + 1):
        start = tile * TILE - AMBIT
        low, high = max(start, 0), min(start + PAD, length)
        out[tile + 1, :, low:high] = FORWARD[:, low - start : high - start]
    return out.reshape(-1, length)


def two_tables(table):
    high = np.asarray(table).astype(jnp.bfloat16)
    return high, (table - high.astype(np.float64)).astype(jnp.bfloat16)


def grid_tables():
    freqs = np.arange(FREQ) - FREQ // 2
    turn = 2.0 * math.pi * (np.arange(GRID)[:, None] * freqs[None, :]) / GRID
    c, s = np.cos(turn) / math.sqrt(FREQ), np.sin(turn) / math.sqrt(FREQ)
    zero = np.zeros((2 * FREQ, 2 * GRID))
    one = np.block([[c.T, s.T], [-s.T, c.T]])
    there_high, there_low = two_tables(np.block([[one, zero], [zero, one]]))
    there = np.concatenate([there_high, there_low], 0)
    high, _ = two_tables(np.concatenate([c, s], 1))
    rows = np.concatenate([high, np.zeros_like(high)], 1)
    rows_back = np.concatenate([high.T, np.zeros_like(high)], 1)
    zero = np.zeros((2 * GRID, 2 * FREQ))
    parts = []
    for adj in (np.block([[c, -s], [s, c]]), np.block([[-s, -c], [c, -s]])):
        parts.append(np.block([[adj, zero], [zero, adj]]))
    back, _ = two_tables(np.concatenate(parts, 0))
    waves = np.arange(-(FREQ - 1), FREQ)
    apart = (np.arange(TILE) + AMBIT)[:, None] / PAD - np.arange(GRID)[None, :] / GRID
    fine = np.cos(2.0 * math.pi * apart[:, :, None] * waves).sum(-1) / GRID
    high, low = two_tables(fine)
    up = np.concatenate([high, high, low, np.zeros_like(low)], 1)
    down = np.concatenate([high.T, low.T], 0)
    down_cols = np.concatenate([high, high, low, low], 1)
    return there, rows, rows_back, back, up, np.ascontiguousarray(up.T), down, down_cols


def exchange_tables(slots):
    rows = spread(slots).reshape(slots + 2, 2, FREQ, -1).transpose(1, 0, 2, 3).reshape(2 * (slots + 2) * FREQ, -1)
    near = spread(1).reshape(3, 2, FREQ, TILE)
    cols = []
    for which in (1, 1, 0, 2):
        c, s = near[which].astype(np.float32)
        cols.append(np.block([[c.T, s.T], [-s.T, c.T]]))
    return rows, np.concatenate(cols, 1).astype(jnp.bfloat16)


def lowering_tables():
    near = spread(1).reshape(3, 2, FREQ, TILE).astype(np.float32)
    full = [np.block([[c, -s], [s, c]]) for c, s in near]
    cut = [np.block([[c, -s], [s, c]]) for c, s in (near[0][:, :, :128], near[2][:, :, -128:])]
    twice = lambda a: np.concatenate([a, a], 0).astype(jnp.bfloat16)
    return twice(full[1]), np.stack([twice(cut[0]), twice(cut[1])])


def mixed_dot(left, right):
    return jnp.dot(left, right, preferred_element_type=jnp.float32)


def two_parts(value):
    high = value.astype(jnp.bfloat16)
    return high, (value - high.astype(jnp.float32)).astype(jnp.bfloat16)


MESH = pl.DeviceIdType.MESH
VMEM = pl.BlockSpec(memory_space=pltpu.VMEM)
NEAR = [(dy, dx) for dy in (-1, 0, 1) for dx in (-1, 0, 1) if (dy, dx) != (0, 0)]


class Place:
    def __init__(self, bands, size):
        self.bands, self.size = bands, size
        self.band, self.column = lax.axis_index("own"), lax.axis_index("img")

    def near(self, dy, dx):
        row, col = self.band + dy, self.column + dx
        there = (row >= 0) & (row < self.bands) & (col >= 0) & (col < self.size)
        return there, (row, col)

    def greet(self):
        barrier = pltpu.get_barrier_semaphore()
        count = jnp.int32(0)
        for offset in NEAR:
            there, device = self.near(*offset)
            count = count + there.astype(jnp.int32)

            @pl.when(there)
            def _():
                pl.semaphore_signal(barrier, inc=1, device_id=device, device_id_type=MESH)

        return lambda: pl.semaphore_wait(barrier, count)


def push(src, dst, send, recv, device):
    return pltpu.make_async_remote_copy(
        src_ref=src, dst_ref=dst, send_sem=send, recv_sem=recv, device_id=device, device_id_type=MESH
    )


def swapped(value, lane):
    return jnp.where(lane % 64 < 32, pltpu.roll(value, 96, 1), pltpu.roll(value, 32, 1))


def spectrum_gradients(m, flags, wanted, kr_ref, ki_ref, t, sens_ref):
    lane = lax.broadcasted_iota(jnp.int32, (FREQ, 128), 1)
    sign = jnp.where(lane % 64 < 32, -1.0, 1.0)
    n = sign * swapped(m, lane)
    parts = []
    for k in range(KERNELS):
        kr, ki = kr_ref[k], ki_ref[k]
        parts += [kr * m + ki * n, kr * n - ki * m]
    high = jnp.concatenate(parts, 0).astype(jnp.bfloat16)
    half = mixed_dot(jnp.concatenate([high, high], 1), t["there"][...]).astype(jnp.bfloat16)
    rows_table, rows_back = t["rows"][:, : 2 * FREQ], t["rows_back"][:, : 2 * FREQ]
    fields = []
    total = jnp.zeros((GRID, 256), jnp.float32)
    for k in range(KERNELS):
        field = mixed_dot(rows_table, half[k * 64 : (k + 1) * 64])
        fields.append(field)
        total = total + field * field
    coarse = jnp.concatenate([total[:, :128], total[:, 128:]], 0)
    coarse = coarse + pltpu.roll(coarse, 64, 1)
    high, low = two_parts(coarse)
    first = lax.broadcasted_iota(jnp.int32, (2 * GRID, 128), 1) < 64
    zero = jnp.zeros((2 * GRID, 128), jnp.float32)
    high32, low32 = high.astype(jnp.float32), low.astype(jnp.float32)
    lhs = jnp.concatenate([jnp.where(first, high32, low32), jnp.where(first, high32, zero)], 1).astype(jnp.bfloat16)
    across = mixed_dot(lhs, t["up_t"][...])
    high, low = two_parts(across)
    rows = 128
    for slot in range(2):
        at = slice(slot * GRID, (slot + 1) * GRID)
        rhs = jnp.concatenate([high[at], low[at], high[at], jnp.zeros((GRID, TILE), jnp.bfloat16)], 0)
        for start in range(0, TILE, rows):
            intensity = mixed_dot(t["up"][start : start + rows, :], rhs)
            bend = jnp.tanh((0.5 * STEEP) * (intensity - THRESHOLD))
            goal = wanted[slot * TILE + start : slot * TILE + start + rows, :].astype(jnp.float32)
            sens = (0.5 * STEEP) * (1.0 + bend - 2.0 * goal) * (1.0 - bend * bend)
            sens_ref[start : start + rows, slot * TILE : (slot + 1) * TILE] = sens.astype(jnp.bfloat16)
    folded = mixed_dot(t["down"][...], sens_ref[...])
    folded = folded[:GRID] + folded[GRID:]
    high, low = two_parts(jnp.concatenate([folded[:, :TILE], folded[:, TILE:]], 0))
    grid = mixed_dot(jnp.concatenate([high, low], 0), t["down_cols"][...])
    grid = grid[:128, :128] + grid[:128, 128:] + grid[128:, :128]
    weight = jnp.concatenate([grid[:GRID], grid[GRID:]], 1)
    tops, bottoms = [], []
    for k in range(KERNELS):
        pulled = mixed_dot(rows_back, (fields[k] * weight).astype(jnp.bfloat16))
        tops.append(pulled[:FREQ])
        bottoms.append(pulled[FREQ:])
    pulled = jnp.concatenate([jnp.concatenate(tops, 0), jnp.concatenate(bottoms, 0)], 1)
    back = mixed_dot(pulled.astype(jnp.bfloat16), t["back"][...])
    sum_r = jnp.zeros((FREQ, 128), jnp.float32)
    sum_i = jnp.zeros((FREQ, 128), jnp.float32)
    for k in range(KERNELS):
        z = back[k * FREQ : (k + 1) * FREQ]
        sum_r = sum_r + kr_ref[k] * z
        sum_i = sum_i + ki_ref[k] * z
    grad = sum_r - sign * swapped(sum_i, lane)
    return jnp.where(jnp.where(lane < 64, flags[0], flags[1]) > 0, grad, 0.0)


def packed(arrays):
    pieces, places, top = [], [], 0
    for name, table in arrays.items():
        height, width = table.shape
        for left in range(0, width, 256):
            piece = table[:, left : left + 256]
            places.append((name, top, height, left, piece.shape[1]))
            pieces.append(np.pad(piece, ((0, 0), (0, 256 - piece.shape[1]))))
            top += height
    return np.concatenate(pieces, 0), places


def all_tables(slots):
    arrays = {}
    arrays["row_table"], arrays["cols"] = exchange_tables(slots)
    names = ["there", "rows", "rows_back", "back", "up", "up_t", "down", "down_cols"]
    grid = dict(zip(names, grid_tables()))
    for name in ("there", "rows", "up_t", "up", "down", "down_cols", "rows_back", "back"):
        arrays[name] = grid[name]
    arrays["own"], beside = lowering_tables()
    arrays["left"], arrays["right"] = beside
    return arrays


def whole(
    bands, size, slots, names, places, root_ref, occ_ref, kern_hbm, mask_hbm, targ_hbm, packed_hbm, low_ref, *refs
):
    count = len(names)
    held = dict(zip(names, refs[:count]))
    (kern_ref, mask_ref, targ_ref, kr_ref, ki_ref, sens_ref, out_msg, side, full, near, copy_sem, table_sem,
     side_send, side_recv, near_send, near_recv) = refs[count:]
    at = Place(bands, size)
    arrived = at.greet()
    copies = []
    for n, (src, dst) in enumerate(((mask_hbm, mask_ref), (kern_hbm, kern_ref), (targ_hbm, targ_ref))):
        copies.append(pltpu.make_async_copy(src, dst, copy_sem.at[n]))
    tables = []
    for n, (name, top, height, left, width) in enumerate(places):
        tables.append(
            pltpu.make_async_copy(
                packed_hbm.at[pl.ds(top, height), pl.ds(0, width)],
                held[name].at[:, pl.ds(left, width)],
                table_sem.at[n],
            )
        )
    early = [c for c, place in zip(tables, places) if place[0] in ("row_table", "cols")]
    late = [c for c, place in zip(tables, places) if place[0] not in ("row_table", "cols")]
    for copy in [copies[0]] + early + copies[1:] + late:
        copy.start()

    for copy in [copies[0]] + early:
        copy.wait()
    upper = mixed_dot(held["row_table"][...], mask_ref[...]).astype(jnp.bfloat16)
    half = (slots + 2) * FREQ
    three = mixed_dot(jnp.concatenate([upper[:half], upper[half:]], 1), held["cols"][...])
    first = lax.broadcasted_iota(jnp.int32, (FREQ, 128), 1) < 64

    def packed_part(dy, dx):
        def rows(tile):
            span = slice((tile + 1) * FREQ, (tile + 2) * FREQ)
            if dx == 0:
                return three[span, :128]
            value = three[span, 128:]
            turned = pltpu.roll(value, 64, 1)
            return jnp.where(first, value, turned) if dx < 0 else jnp.where(first, turned, value)

        if dy == 0:
            return jnp.where(first, rows(0), rows(1))
        return jnp.where(first, 0.0, rows(-1)) if dy < 0 else jnp.where(first, rows(slots), 0.0)

    spectrum = packed_part(0, 0)
    for n, offset in enumerate(NEAR):
        out_msg[n] = packed_part(*offset)
    arrived()

    def spread_out(sources, into, send, recv):
        sent = []
        for n, offset in enumerate(NEAR):
            there, device = at.near(*offset)
            copy = push(sources[n], into.at[n], send.at[n], recv.at[n], device)
            sent.append((there, copy))
            pl.when(there)(copy.start)
        return sent

    def take_in(sent, into):
        for n, (dy, dx) in enumerate(NEAR):
            source, _ = at.near(-dy, -dx)
            pl.when(source)(sent[n][1].wait_recv)

            @pl.when(jnp.logical_not(source))
            def _():
                into[n] = jnp.zeros((FREQ, 128), jnp.float32)

    parts_sent = spread_out([out_msg.at[n] for n in range(len(NEAR))], side, side_send, side_recv)
    copies[1].wait()
    for k in range(KERNELS):
        root = jnp.sqrt(jnp.full((1, 128), root_ref[k], jnp.float32))
        for part, ref in ((0, kr_ref), (1, ki_ref)):
            ref[k] = jnp.concatenate([kern_ref[part, k]] * 4, 1) * root
    for copy in copies[2:] + late:
        copy.wait()
    flags = [occ_ref[at.band * slots + slot, at.column] for slot in range(slots)]
    take_in(parts_sent, side)
    for n in range(len(NEAR)):
        spectrum = spectrum + side[n]
    total = spectrum_gradients(spectrum, flags, targ_ref, kr_ref, ki_ref, held, sens_ref)
    full[...] = total
    sent = spread_out([full] * len(NEAR), near, near_send, near_recv)
    take_in(sent, near)

    def product(dx, table):
        get = lambda dy: total if (dy, dx) == (0, 0) else near[NEAR.index((-dy, -dx))]
        upper, middle, lower = get(-1), get(0), get(1)
        stack = [
            jnp.where(first, 0.0, upper), jnp.where(first, middle, 0.0),
            jnp.where(first, 0.0, middle), jnp.where(first, lower, 0.0),
        ]
        high, low = two_parts(jnp.concatenate(stack, 0))
        return mixed_dot(high, table) + mixed_dot(low, table)

    own = product(0, held["own"][...])
    left = product(-1, held["left"][...])
    right = product(1, held["right"][...])
    for part in range(2):
        value = own[:, part * TILE : (part + 1) * TILE]
        span = slice(part * 128, part * 128 + 128)
        value = jnp.concatenate(
            [value[:, :128] + left[:, span], value[:, 128:-128], value[:, -128:] + right[:, span]], 1
        ).astype(jnp.bfloat16)
        for tile in range(slots + 2):
            low_ref[(2 * tile + part) * FREQ : (2 * tile + part + 1) * FREQ, :] = value[
                tile * FREQ : (tile + 1) * FREQ
            ]
    for there, copy in parts_sent + sent:
        pl.when(there)(copy.wait_send)


def whole_call(mask_field, target_field, occupancy, kernels, weights, bands, size, slots):
    arrays = all_tables(slots)
    tables, places = packed(arrays)
    dma = pltpu.SemaphoreType.DMA
    smem, hbm = pl.BlockSpec(memory_space=pltpu.SMEM), pl.BlockSpec(memory_space=pl.ANY)
    message = pltpu.VMEM((len(NEAR), FREQ, 128), jnp.float32)
    spectra = pltpu.VMEM((KERNELS, FREQ, 128), jnp.float32)
    return pl.pallas_call(
        lambda *refs: whole(bands, size, slots, list(arrays), places, *refs),
        out_shape=jax.ShapeDtypeStruct(((slots + 2) * 2 * FREQ, TILE), jnp.bfloat16),
        in_specs=[smem, smem, hbm, hbm, hbm, hbm],
        out_specs=VMEM,
        scratch_shapes=[pltpu.VMEM(a.shape, jnp.bfloat16) for a in arrays.values()]
        + [
            pltpu.VMEM(kernels.shape, kernels.dtype),
            pltpu.VMEM(mask_field.shape, mask_field.dtype),
            pltpu.VMEM(target_field.shape, target_field.dtype),
            spectra, spectra,
            pltpu.VMEM((TILE, slots * TILE), jnp.bfloat16),
            message, message,
            pltpu.VMEM((FREQ, 128), jnp.float32),
            message,
            dma((3,)), dma((len(places),)),
            dma((len(NEAR),)), dma((len(NEAR),)), dma((len(NEAR),)), dma((len(NEAR),)),
        ],
        compiler_params=pltpu.CompilerParams(
            collective_id=0, has_side_effects=True, vmem_limit_bytes=VMEM_GRANT
        ),
    )(weights, occupancy, kernels, mask_field, target_field, jnp.asarray(tables))


def finish_call(lowered, mask_field, slots):
    table = jnp.asarray(np.ascontiguousarray(spread(slots).T))
    height, width = mask_field.shape
    rows = 128
    steps = height // rows

    def finish(table_ref, low_ref, mask_ref, out_ref, held, sems):
        copies = []
        for step in range(steps):
            span = pl.ds(step * rows, rows)
            values = mask_ref[span, :].astype(jnp.float32)
            penalty = GAMMA * 4.0 * values * (values * values - 1.0)
            held[span, :] = mixed_dot(table_ref[span, :], low_ref[...]) + penalty
            copies.append(pltpu.make_async_copy(held.at[span], out_ref.at[span], sems.at[step]))
            copies[-1].start()
        for copy in copies:
            copy.wait()

    return pl.pallas_call(
        finish,
        out_shape=jax.ShapeDtypeStruct((height, width), jnp.float32),
        in_specs=[VMEM, VMEM, VMEM],
        out_specs=pl.BlockSpec(memory_space=pl.ANY),
        scratch_shapes=[pltpu.VMEM((height, width), jnp.float32), pltpu.SemaphoreType.DMA((steps,))],
        compiler_params=pltpu.CompilerParams(vmem_limit_bytes=16 * 1024 * 1024),
    )(table, lowered, mask_field)


def on_device(mask_field, target_field, occupancy, kernels, weights):
    slots = mask_field.shape[0] // TILE
    bands, size = lax.axis_size("own"), lax.axis_size("img")
    assert slots == 2
    lowered = whole_call(mask_field, target_field, occupancy, kernels, weights, bands, size, slots)
    return finish_call(lowered, mask_field, slots)


def solution(mesh):
    return jax.shard_map(
        on_device,
        mesh=mesh,
        in_specs=(P("own", "img"), P("own", "img"), P(), P(), P()),
        out_specs=P("own", "img"),
        check_vma=False,
    )
```

```python
import math

import jax
import jax.numpy as jnp
import numpy as np
from jax import lax
from jax.experimental import pallas as pl
from jax.experimental.pallas import tpu as pltpu
from jax.sharding import PartitionSpec as P

TILE = 512
AMBIT = 64
FREQ = 32
KERNELS = 24
PAD = 640
STEEP = 2.0
THRESHOLD = 1.5
GAMMA = 0.25
VMEM_GRANT = 61 * 1024 * 1024
PIECES = 4
GRID = 64


def tables():
    freqs = np.arange(FREQ) - FREQ // 2
    turn = np.float32(2.0 * math.pi / PAD)
    phase = ((freqs[:, None] * np.arange(PAD)[None, :]) % PAD).astype(np.float32) * turn
    bf = lambda a: np.asarray(a, np.float32).astype(jnp.bfloat16)
    return (
        bf(np.cos(phase) / np.float32(math.sqrt(PAD))),
        bf(-np.sin(phase) / np.float32(math.sqrt(PAD))),
    )


FC, FS = tables()
FORWARD = np.concatenate([FC, FS], 0)


def spread(count):
    length = count * TILE
    out = np.zeros((count + 2, 2 * FREQ, length), jnp.bfloat16)
    for tile in range(-1, count + 1):
        start = tile * TILE - AMBIT
        low, high = max(start, 0), min(start + PAD, length)
        out[tile + 1, :, low:high] = FORWARD[:, low - start : high - start]
    return out.reshape(-1, length)


def two_tables(table):
    high = np.asarray(table).astype(jnp.bfloat16)
    return high, (table - high.astype(np.float64)).astype(jnp.bfloat16)


def grid_tables():
    freqs = np.arange(FREQ) - FREQ // 2
    turn = 2.0 * math.pi * (np.arange(GRID)[:, None] * freqs[None, :]) / GRID
    c, s = np.cos(turn) / math.sqrt(FREQ), np.sin(turn) / math.sqrt(FREQ)
    zero = np.zeros((2 * FREQ, 2 * GRID))
    one = np.block([[c.T, s.T], [-s.T, c.T]])
    there_high, there_low = two_tables(np.block([[one, zero], [zero, one]]))
    there = np.concatenate([there_high, there_low], 0)
    high, _ = two_tables(np.concatenate([c, s], 1))
    rows = np.concatenate([high, np.zeros_like(high)], 1)
    rows_back = np.concatenate([high.T, np.zeros_like(high)], 1)
    zero = np.zeros((2 * GRID, 2 * FREQ))
    parts = []
    for adj in (np.block([[c, -s], [s, c]]), np.block([[-s, -c], [c, -s]])):
        parts.append(np.block([[adj, zero], [zero, adj]]))
    back, _ = two_tables(np.concatenate(parts, 0))
    waves = np.arange(-(FREQ - 1), FREQ)
    apart = (np.arange(TILE) + AMBIT)[:, None] / PAD - np.arange(GRID)[None, :] / GRID
    fine = np.cos(2.0 * math.pi * apart[:, :, None] * waves).sum(-1) / GRID
    high, low = two_tables(fine)
    up = np.concatenate([high, high, low, np.zeros_like(low)], 1)
    down = np.concatenate([high.T, low.T], 0)
    down_cols = np.concatenate([high, high, low, low], 1)
    return there, rows, rows_back, back, up, np.ascontiguousarray(up.T), down, down_cols


def exchange_tables(slots):
    rows = spread(slots).reshape(slots + 2, 2, FREQ, -1).transpose(1, 0, 2, 3).reshape(2 * (slots + 2) * FREQ, -1)
    near = spread(1).reshape(3, 2, FREQ, TILE)
    cols = []
    for which in (1, 1, 0, 2):
        c, s = near[which].astype(np.float32)
        cols.append(np.block([[c.T, s.T], [-s.T, c.T]]))
    return rows, np.concatenate(cols, 1).astype(jnp.bfloat16)


def lowering_tables():
    near = spread(1).reshape(3, 2, FREQ, TILE).astype(np.float32)
    full = [np.block([[c, -s], [s, c]]) for c, s in near]
    cut = [np.block([[c, -s], [s, c]]) for c, s in (near[0][:, :, :128], near[2][:, :, -128:])]
    twice = lambda a: np.concatenate([a, a], 0).astype(jnp.bfloat16)
    return twice(full[1]), np.stack([twice(cut[0]), twice(cut[1])])


def mixed_dot(left, right):
    return jnp.dot(left, right, preferred_element_type=jnp.float32)


def two_parts(value):
    high = value.astype(jnp.bfloat16)
    return high, (value - high.astype(jnp.float32)).astype(jnp.bfloat16)


MESH = pl.DeviceIdType.MESH
VMEM = pl.BlockSpec(memory_space=pltpu.VMEM)
NEAR = [(dy, dx) for dy in (-1, 0, 1) for dx in (-1, 0, 1) if (dy, dx) != (0, 0)]


class Place:
    def __init__(self, bands, size):
        self.bands, self.size = bands, size
        self.band, self.column = lax.axis_index("own"), lax.axis_index("img")

    def near(self, dy, dx):
        row, col = self.band + dy, self.column + dx
        there = (row >= 0) & (row < self.bands) & (col >= 0) & (col < self.size)
        return there, (row, col)

    def greet(self):
        barrier = pltpu.get_barrier_semaphore()
        count = jnp.int32(0)
        for offset in NEAR:
            there, device = self.near(*offset)
            count = count + there.astype(jnp.int32)

            @pl.when(there)
            def _():
                pl.semaphore_signal(barrier, inc=1, device_id=device, device_id_type=MESH)

        return lambda: pl.semaphore_wait(barrier, count)


def push(src, dst, send, recv, device):
    return pltpu.make_async_remote_copy(
        src_ref=src, dst_ref=dst, send_sem=send, recv_sem=recv, device_id=device, device_id_type=MESH
    )


def swapped(value, lane):
    return jnp.where(lane % 64 < 32, pltpu.roll(value, 96, 1), pltpu.roll(value, 32, 1))


def spectrum_gradients(m, flags, wanted, kr_ref, ki_ref, t, sens_ref):
    lane = lax.broadcasted_iota(jnp.int32, (FREQ, 128), 1)
    sign = jnp.where(lane % 64 < 32, -1.0, 1.0)
    n = sign * swapped(m, lane)
    parts = []
    for k in range(KERNELS):
        kr, ki = kr_ref[k], ki_ref[k]
        parts += [kr * m + ki * n, kr * n - ki * m]
    high = jnp.concatenate(parts, 0).astype(jnp.bfloat16)
    half = mixed_dot(jnp.concatenate([high, high], 1), t["there"][...]).astype(jnp.bfloat16)
    rows_table, rows_back = t["rows"][:, : 2 * FREQ], t["rows_back"][:, : 2 * FREQ]
    fields = []
    total = jnp.zeros((GRID, 256), jnp.float32)
    for k in range(KERNELS):
        field = mixed_dot(rows_table, half[k * 64 : (k + 1) * 64])
        fields.append(field)
        total = total + field * field
    coarse = jnp.concatenate([total[:, :128], total[:, 128:]], 0)
    coarse = coarse + pltpu.roll(coarse, 64, 1)
    high, low = two_parts(coarse)
    first = lax.broadcasted_iota(jnp.int32, (2 * GRID, 128), 1) < 64
    zero = jnp.zeros((2 * GRID, 128), jnp.float32)
    high32, low32 = high.astype(jnp.float32), low.astype(jnp.float32)
    lhs = jnp.concatenate([jnp.where(first, high32, low32), jnp.where(first, high32, zero)], 1).astype(jnp.bfloat16)
    across = mixed_dot(lhs, t["up_t"][...])
    high, low = two_parts(across)
    rows = 256
    for slot in range(2):
        at = slice(slot * GRID, (slot + 1) * GRID)
        rhs = jnp.concatenate([high[at], low[at], high[at], jnp.zeros((GRID, TILE), jnp.bfloat16)], 0)
        for start in range(0, TILE, rows):
            intensity = mixed_dot(t["up"][start : start + rows, :], rhs)
            bend = jnp.tanh((0.5 * STEEP) * (intensity - THRESHOLD))
            goal = wanted[slot * TILE + start : slot * TILE + start + rows, :].astype(jnp.float32)
            sens = (0.5 * STEEP) * (1.0 + bend - 2.0 * goal) * (1.0 - bend * bend)
            sens_ref[start : start + rows, slot * TILE : (slot + 1) * TILE] = sens.astype(jnp.bfloat16)
    folded = mixed_dot(t["down"][...], sens_ref[...])
    folded = folded[:GRID] + folded[GRID:]
    high, low = two_parts(jnp.concatenate([folded[:, :TILE], folded[:, TILE:]], 0))
    grid = mixed_dot(jnp.concatenate([high, low], 0), t["down_cols"][...])
    grid = grid[:128, :128] + grid[:128, 128:] + grid[128:, :128]
    weight = jnp.concatenate([grid[:GRID], grid[GRID:]], 1)
    tops, bottoms = [], []
    for k in range(KERNELS):
        pulled = mixed_dot(rows_back, (fields[k] * weight).astype(jnp.bfloat16))
        tops.append(pulled[:FREQ])
        bottoms.append(pulled[FREQ:])
    pulled = jnp.concatenate([jnp.concatenate(tops, 0), jnp.concatenate(bottoms, 0)], 1)
    back = mixed_dot(pulled.astype(jnp.bfloat16), t["back"][...])
    sum_r = jnp.zeros((FREQ, 128), jnp.float32)
    sum_i = jnp.zeros((FREQ, 128), jnp.float32)
    for k in range(KERNELS):
        z = back[k * FREQ : (k + 1) * FREQ]
        sum_r = sum_r + kr_ref[k] * z
        sum_i = sum_i + ki_ref[k] * z
    grad = sum_r - sign * swapped(sum_i, lane)
    return jnp.where(jnp.where(lane < 64, flags[0], flags[1]) > 0, grad, 0.0)


def packed(arrays):
    pieces, places, top = [], [], 0
    for name, table in arrays.items():
        height, width = table.shape
        for left in range(0, width, 256):
            piece = table[:, left : left + 256]
            places.append((name, top, height, left, piece.shape[1]))
            pieces.append(np.pad(piece, ((0, 0), (0, 256 - piece.shape[1]))))
            top += height
    return np.concatenate(pieces, 0), places


def all_tables(slots):
    arrays = {}
    arrays["row_table"], arrays["cols"] = exchange_tables(slots)
    names = ["there", "rows", "rows_back", "back", "up", "up_t", "down", "down_cols"]
    grid = dict(zip(names, grid_tables()))
    for name in ("there", "rows", "up_t", "up", "down", "down_cols", "rows_back", "back"):
        arrays[name] = grid[name]
    arrays["own"], beside = lowering_tables()
    arrays["left"], arrays["right"] = beside
    return arrays


def whole(
    bands, size, slots, names, places, root_hbm, occ_hbm, kern_hbm, mask_hbm, targ_hbm, packed_hbm, low_ref, *refs
):
    count = len(names)
    held = dict(zip(names, refs[:count]))
    (root_ref, occ_ref, kern_ref, mask_ref, targ_ref, kr_ref, ki_ref, sens_ref, out_msg, side, full, near, copy_sem, table_sem,
     side_send, side_recv, near_send, near_recv) = refs[count:]
    at = Place(bands, size)
    arrived = at.greet()
    copies = []
    pairs = [(root_hbm, root_ref), (occ_hbm, occ_ref), (kern_hbm, kern_ref), (targ_hbm, targ_ref)]
    piece = slots * TILE // PIECES
    for n in range(PIECES):
        span = pl.ds(n * piece, piece)
        pairs.append((mask_hbm.at[span], mask_ref.at[span]))
    for n, (src, dst) in enumerate(pairs):
        copies.append(pltpu.make_async_copy(src, dst, copy_sem.at[n]))
    mask_copies, copies = copies[4:], copies[:4]
    tables = []
    for n, (name, top, height, left, width) in enumerate(places):
        tables.append(
            pltpu.make_async_copy(
                packed_hbm.at[pl.ds(top, height), pl.ds(0, width)],
                held[name].at[:, pl.ds(left, width)],
                table_sem.at[n],
            )
        )
    early = [c for c, place in zip(tables, places) if place[0] in ("row_table", "cols")]
    late = [c for c, place in zip(tables, places) if place[0] not in ("row_table", "cols")]
    for copy in mask_copies + early + copies + late:
        copy.start()

    for copy in mask_copies + early:
        copy.wait()
    upper = mixed_dot(held["row_table"][...], mask_ref[...]).astype(jnp.bfloat16)
    half = (slots + 2) * FREQ
    three = mixed_dot(jnp.concatenate([upper[:half], upper[half:]], 1), held["cols"][...])
    first = lax.broadcasted_iota(jnp.int32, (FREQ, 128), 1) < 64

    def packed_part(dy, dx):
        def rows(tile):
            span = slice((tile + 1) * FREQ, (tile + 2) * FREQ)
            if dx == 0:
                return three[span, :128]
            value = three[span, 128:]
            turned = pltpu.roll(value, 64, 1)
            return jnp.where(first, value, turned) if dx < 0 else jnp.where(first, turned, value)

        if dy == 0:
            return jnp.where(first, rows(0), rows(1))
        return jnp.where(first, 0.0, rows(-1)) if dy < 0 else jnp.where(first, rows(slots), 0.0)

    spectrum = packed_part(0, 0)
    for n, offset in enumerate(NEAR):
        out_msg[n] = packed_part(*offset)
    arrived()

    def spread_out(sources, into, send, recv):
        sent = []
        for n, offset in enumerate(NEAR):
            there, device = at.near(*offset)
            copy = push(sources[n], into.at[n], send.at[n], recv.at[n], device)
            sent.append((there, copy))
            pl.when(there)(copy.start)
        return sent

    def take_in(sent, into):
        for n, (dy, dx) in enumerate(NEAR):
            source, _ = at.near(-dy, -dx)
            pl.when(source)(sent[n][1].wait_recv)

            @pl.when(jnp.logical_not(source))
            def _():
                into[n] = jnp.zeros((FREQ, 128), jnp.float32)

    parts_sent = spread_out([out_msg.at[n] for n in range(len(NEAR))], side, side_send, side_recv)
    for copy in copies[:3]:
        copy.wait()
    for k in range(KERNELS):
        root = jnp.sqrt(jnp.full((1, 128), root_ref[k], jnp.float32))
        for part, ref in ((0, kr_ref), (1, ki_ref)):
            ref[k] = jnp.concatenate([kern_ref[part, k]] * 4, 1) * root
    for copy in copies[3:] + late:
        copy.wait()
    flags = [occ_ref[at.band * slots + slot, at.column] for slot in range(slots)]
    take_in(parts_sent, side)
    for n in range(len(NEAR)):
        spectrum = spectrum + side[n]
    total = spectrum_gradients(spectrum, flags, targ_ref, kr_ref, ki_ref, held, sens_ref)
    full[...] = total
    sent = spread_out([full] * len(NEAR), near, near_send, near_recv)

    def product(stack, table):
        high, low = two_parts(jnp.concatenate(stack, 0))
        table = table[...]
        return mixed_dot(jnp.concatenate([high, low], 1), jnp.concatenate([table, table], 0))

    def halves(value):
        return [jnp.where(first, value, 0.0), jnp.where(first, 0.0, value)]

    middle = product(halves(total), held["own"])
    take_in(sent, near)

    def get(dy, dx):
        return near[NEAR.index((-dy, -dx))]

    def beside(dx, table):
        outer = [jnp.where(first, 0.0, get(-1, dx)), jnp.where(first, get(1, dx), 0.0)]
        return product([outer[0]] + halves(get(0, dx)) + [outer[1]], table)

    outer = product([jnp.where(first, 0.0, get(-1, 0)), jnp.where(first, get(1, 0), 0.0)], held["own"])
    left, right = beside(-1, held["left"]), beside(1, held["right"])
    own = jnp.concatenate([outer[:FREQ], middle, outer[FREQ:]], 0)
    for part in range(2):
        value = own[:, part * TILE : (part + 1) * TILE]
        span = slice(part * 128, part * 128 + 128)
        value = jnp.concatenate(
            [value[:, :128] + left[:, span], value[:, 128:-128], value[:, -128:] + right[:, span]], 1
        ).astype(jnp.bfloat16)
        for tile in range(slots + 2):
            low_ref[(2 * tile + part) * FREQ : (2 * tile + part + 1) * FREQ, :] = value[
                tile * FREQ : (tile + 1) * FREQ
            ]
    for there, copy in parts_sent + sent:
        pl.when(there)(copy.wait_send)


def whole_call(mask_field, target_field, occupancy, kernels, weights, bands, size, slots):
    arrays = all_tables(slots)
    tables, places = packed(arrays)
    dma = pltpu.SemaphoreType.DMA
    hbm = pl.BlockSpec(memory_space=pl.ANY)
    message = pltpu.VMEM((len(NEAR), FREQ, 128), jnp.float32)
    spectra = pltpu.VMEM((KERNELS, FREQ, 128), jnp.float32)
    return pl.pallas_call(
        lambda *refs: whole(bands, size, slots, list(arrays), places, *refs),
        out_shape=jax.ShapeDtypeStruct(((slots + 2) * 2 * FREQ, TILE), jnp.bfloat16),
        in_specs=[hbm] * 6,
        out_specs=VMEM,
        scratch_shapes=[pltpu.VMEM(a.shape, jnp.bfloat16) for a in arrays.values()]
        + [
            pltpu.SMEM(weights.shape, weights.dtype),
            pltpu.SMEM(occupancy.shape, occupancy.dtype),
            pltpu.VMEM(kernels.shape, kernels.dtype),
            pltpu.VMEM(mask_field.shape, mask_field.dtype),
            pltpu.VMEM(target_field.shape, target_field.dtype),
            spectra, spectra,
            pltpu.VMEM((TILE, slots * TILE), jnp.bfloat16),
            message, message,
            pltpu.VMEM((FREQ, 128), jnp.float32),
            message,
            dma((4 + PIECES,)), dma((len(places),)),
            dma((len(NEAR),)), dma((len(NEAR),)), dma((len(NEAR),)), dma((len(NEAR),)),
        ],
        compiler_params=pltpu.CompilerParams(
            collective_id=0, has_side_effects=True, vmem_limit_bytes=VMEM_GRANT
        ),
    )(weights, occupancy, kernels, mask_field, target_field, jnp.asarray(tables))


def finish_call(lowered, mask_field, slots):
    table = jnp.asarray(np.ascontiguousarray(spread(slots).T))
    height, width = mask_field.shape
    rows = 256
    steps = height // rows

    def finish(table_ref, low_hbm, mask_ref, out_ref, low_ref, held, low_sem, sems):
        fetch = pltpu.make_async_copy(low_hbm, low_ref, low_sem)
        fetch.start()
        values = mask_ref[...].astype(jnp.float32)
        held[...] = GAMMA * 4.0 * values * (values * values - 1.0)
        fetch.wait()
        copies = []
        for step in range(steps):
            span = pl.ds(step * rows, rows)
            held[span, :] = held[span, :] + mixed_dot(table_ref[span, :], low_ref[...])
            copies.append(pltpu.make_async_copy(held.at[span], out_ref.at[span], sems.at[step]))
            copies[-1].start()
        for copy in copies:
            copy.wait()

    return pl.pallas_call(
        finish,
        out_shape=jax.ShapeDtypeStruct((height, width), jnp.float32),
        in_specs=[VMEM, pl.BlockSpec(memory_space=pl.ANY), VMEM],
        out_specs=pl.BlockSpec(memory_space=pl.ANY),
        scratch_shapes=[
            pltpu.VMEM(lowered.shape, lowered.dtype),
            pltpu.VMEM((height, width), jnp.float32),
            pltpu.SemaphoreType.DMA,
            pltpu.SemaphoreType.DMA((steps,)),
        ],
        compiler_params=pltpu.CompilerParams(vmem_limit_bytes=VMEM_GRANT),
    )(table, lowered, mask_field)


def on_device(mask_field, target_field, occupancy, kernels, weights):
    slots = mask_field.shape[0] // TILE
    bands, size = lax.axis_size("own"), lax.axis_size("img")
    assert slots == 2
    lowered = whole_call(mask_field, target_field, occupancy, kernels, weights, bands, size, slots)
    return finish_call(lowered, mask_field, slots)


def solution(mesh):
    return jax.shard_map(
        on_device,
        mesh=mesh,
        in_specs=(P("own", "img"), P("own", "img"), P(), P(), P()),
        out_specs=P("own", "img"),
        check_vma=False,
    )
```

```python
import math

import jax
import jax.numpy as jnp
import numpy as np
from jax import lax
from jax.experimental import pallas as pl
from jax.experimental.pallas import tpu as pltpu
from jax.sharding import PartitionSpec as P

TILE = 512
AMBIT = 64
FREQ = 32
KERNELS = 24
PAD = 640
STEEP = 2.0
THRESHOLD = 1.5
GAMMA = 0.25
VMEM_GRANT = 107 * 512 * 1024
PIECES = 4
GRID = 64


def tables():
    freqs = np.arange(FREQ) - FREQ // 2
    turn = np.float32(2.0 * math.pi / PAD)
    phase = ((freqs[:, None] * np.arange(PAD)[None, :]) % PAD).astype(np.float32) * turn
    bf = lambda a: np.asarray(a, np.float32).astype(jnp.bfloat16)
    return (
        bf(np.cos(phase) / np.float32(math.sqrt(PAD))),
        bf(-np.sin(phase) / np.float32(math.sqrt(PAD))),
    )


FC, FS = tables()
FORWARD = np.concatenate([FC, FS], 0)


def spread(count):
    length = count * TILE
    out = np.zeros((count + 2, 2 * FREQ, length), jnp.bfloat16)
    for tile in range(-1, count + 1):
        start = tile * TILE - AMBIT
        low, high = max(start, 0), min(start + PAD, length)
        out[tile + 1, :, low:high] = FORWARD[:, low - start : high - start]
    return out.reshape(-1, length)


def two_tables(table):
    high = np.asarray(table).astype(jnp.bfloat16)
    return high, (table - high.astype(np.float64)).astype(jnp.bfloat16)


def grid_tables():
    freqs = np.arange(FREQ) - FREQ // 2
    turn = 2.0 * math.pi * (np.arange(GRID)[:, None] * freqs[None, :]) / GRID
    c, s = np.cos(turn) / math.sqrt(FREQ), np.sin(turn) / math.sqrt(FREQ)
    zero = np.zeros((2 * FREQ, 2 * GRID))
    one = np.block([[c.T, s.T], [-s.T, c.T]])
    there_high, there_low = two_tables(np.block([[one, zero], [zero, one]]))
    there = np.concatenate([there_high, there_low], 0)
    high, _ = two_tables(np.concatenate([c, s], 1))
    rows = np.concatenate([high, np.zeros_like(high)], 1)
    rows_back = np.concatenate([high.T, np.zeros_like(high)], 1)
    zero = np.zeros((2 * GRID, 2 * FREQ))
    parts = []
    for adj in (np.block([[c, -s], [s, c]]), np.block([[-s, -c], [c, -s]])):
        parts.append(np.block([[adj, zero], [zero, adj]]))
    back, _ = two_tables(np.concatenate(parts, 0))
    waves = np.arange(-(FREQ - 1), FREQ)
    apart = (np.arange(TILE) + AMBIT)[:, None] / PAD - np.arange(GRID)[None, :] / GRID
    fine = np.cos(2.0 * math.pi * apart[:, :, None] * waves).sum(-1) / GRID
    high, low = two_tables(fine)
    up = np.concatenate([high, high, low, np.zeros_like(low)], 1)
    down = np.concatenate([high.T, low.T], 0)
    down_cols = np.concatenate([high, high, low, low], 1)
    return there, rows, rows_back, back, up, np.ascontiguousarray(up.T), down, down_cols


def exchange_tables(slots):
    rows = spread(slots).reshape(slots + 2, 2, FREQ, -1).transpose(1, 0, 2, 3).reshape(2 * (slots + 2) * FREQ, -1)
    near = spread(1).reshape(3, 2, FREQ, TILE)
    cols = []
    for which in (1, 1, 0, 2):
        c, s = near[which].astype(np.float32)
        cols.append(np.block([[c.T, s.T], [-s.T, c.T]]))
    return rows, np.concatenate(cols, 1).astype(jnp.bfloat16)


def lowering_tables():
    near = spread(1).reshape(3, 2, FREQ, TILE).astype(np.float32)
    full = [np.block([[c, -s], [s, c]]) for c, s in near]
    cut = [np.block([[c, -s], [s, c]]) for c, s in (near[0][:, :, :128], near[2][:, :, -128:])]
    twice = lambda a: np.concatenate([a, a], 0).astype(jnp.bfloat16)
    return twice(full[1]), np.stack([twice(cut[0]), twice(cut[1])])


def mixed_dot(left, right):
    return jnp.dot(left, right, preferred_element_type=jnp.float32)


def two_parts(value):
    high = value.astype(jnp.bfloat16)
    return high, (value - high.astype(jnp.float32)).astype(jnp.bfloat16)


MESH = pl.DeviceIdType.MESH
VMEM = pl.BlockSpec(memory_space=pltpu.VMEM)
NEAR = [(dy, dx) for dy in (-1, 0, 1) for dx in (-1, 0, 1) if (dy, dx) != (0, 0)]


class Place:
    def __init__(self, bands, size):
        self.bands, self.size = bands, size
        self.band, self.column = lax.axis_index("own"), lax.axis_index("img")

    def near(self, dy, dx):
        row, col = self.band + dy, self.column + dx
        there = (row >= 0) & (row < self.bands) & (col >= 0) & (col < self.size)
        return there, (row, col)

    def greet(self):
        barrier = pltpu.get_barrier_semaphore()
        count = jnp.int32(0)
        for offset in NEAR:
            there, device = self.near(*offset)
            count = count + there.astype(jnp.int32)

            @pl.when(there)
            def _():
                pl.semaphore_signal(barrier, inc=1, device_id=device, device_id_type=MESH)

        return lambda: pl.semaphore_wait(barrier, count)


def push(src, dst, send, recv, device):
    return pltpu.make_async_remote_copy(
        src_ref=src, dst_ref=dst, send_sem=send, recv_sem=recv, device_id=device, device_id_type=MESH
    )


def swapped(value, lane):
    return jnp.where(lane % 64 < 32, pltpu.roll(value, 96, 1), pltpu.roll(value, 32, 1))


def spectrum_gradients(m, flags, wanted, kr_ref, ki_ref, t, sens_ref):
    lane = lax.broadcasted_iota(jnp.int32, (FREQ, 128), 1)
    sign = jnp.where(lane % 64 < 32, -1.0, 1.0)
    n = sign * swapped(m, lane)
    parts = []
    for k in range(KERNELS):
        kr, ki = kr_ref[k], ki_ref[k]
        parts += [kr * m + ki * n, kr * n - ki * m]
    high = jnp.concatenate(parts, 0).astype(jnp.bfloat16)
    half = mixed_dot(jnp.concatenate([high, high], 1), t["there"][...]).astype(jnp.bfloat16)
    rows_table, rows_back = t["rows"][:, : 2 * FREQ], t["rows_back"][:, : 2 * FREQ]
    fields = []
    total = jnp.zeros((GRID, 256), jnp.float32)
    for k in range(KERNELS):
        field = mixed_dot(rows_table, half[k * 64 : (k + 1) * 64])
        fields.append(field)
        total = total + field * field
    coarse = jnp.concatenate([total[:, :128], total[:, 128:]], 0)
    coarse = coarse + pltpu.roll(coarse, 64, 1)
    high, low = two_parts(coarse)
    first = lax.broadcasted_iota(jnp.int32, (2 * GRID, 128), 1) < 64
    zero = jnp.zeros((2 * GRID, 128), jnp.float32)
    high32, low32 = high.astype(jnp.float32), low.astype(jnp.float32)
    lhs = jnp.concatenate([jnp.where(first, high32, low32), jnp.where(first, high32, zero)], 1).astype(jnp.bfloat16)
    across = mixed_dot(lhs, t["up_t"][...])
    high, low = two_parts(across)
    rows = 256
    for slot in range(2):
        at = slice(slot * GRID, (slot + 1) * GRID)
        rhs = jnp.concatenate([high[at], low[at], high[at], jnp.zeros((GRID, TILE), jnp.bfloat16)], 0)
        for start in range(0, TILE, rows):
            intensity = mixed_dot(t["up"][start : start + rows, :], rhs)
            bend = jnp.tanh((0.5 * STEEP) * (intensity - THRESHOLD))
            goal = wanted[slot * TILE + start : slot * TILE + start + rows, :].astype(jnp.float32)
            sens = (0.5 * STEEP) * (1.0 + bend - 2.0 * goal) * (1.0 - bend * bend)
            sens_ref[start : start + rows, slot * TILE : (slot + 1) * TILE] = sens.astype(jnp.bfloat16)
    folded = mixed_dot(t["down"][...], sens_ref[...])
    folded = folded[:GRID] + folded[GRID:]
    high, low = two_parts(jnp.concatenate([folded[:, :TILE], folded[:, TILE:]], 0))
    grid = mixed_dot(jnp.concatenate([high, low], 0), t["down_cols"][...])
    grid = grid[:128, :128] + grid[:128, 128:] + grid[128:, :128]
    weight = jnp.concatenate([grid[:GRID], grid[GRID:]], 1)
    tops, bottoms = [], []
    for k in range(KERNELS):
        pulled = mixed_dot(rows_back, (fields[k] * weight).astype(jnp.bfloat16))
        tops.append(pulled[:FREQ])
        bottoms.append(pulled[FREQ:])
    pulled = jnp.concatenate([jnp.concatenate(tops, 0), jnp.concatenate(bottoms, 0)], 1)
    back = mixed_dot(pulled.astype(jnp.bfloat16), t["back"][...])
    sum_r = jnp.zeros((FREQ, 128), jnp.float32)
    sum_i = jnp.zeros((FREQ, 128), jnp.float32)
    for k in range(KERNELS):
        z = back[k * FREQ : (k + 1) * FREQ]
        sum_r = sum_r + kr_ref[k] * z
        sum_i = sum_i + ki_ref[k] * z
    grad = sum_r - sign * swapped(sum_i, lane)
    return jnp.where(jnp.where(lane < 64, flags[0], flags[1]) > 0, grad, 0.0)


def packed(arrays):
    pieces, places, top = [], [], 0
    for name, table in arrays.items():
        height, width = table.shape
        for left in range(0, width, 256):
            piece = table[:, left : left + 256]
            places.append((name, top, height, left, piece.shape[1]))
            pieces.append(np.pad(piece, ((0, 0), (0, 256 - piece.shape[1]))))
            top += height
    return np.concatenate(pieces, 0), places


def all_tables(slots):
    arrays = {}
    arrays["row_table"], arrays["cols"] = exchange_tables(slots)
    names = ["there", "rows", "rows_back", "back", "up", "up_t", "down", "down_cols"]
    grid = dict(zip(names, grid_tables()))
    for name in ("there", "rows", "up_t", "up", "down", "down_cols", "rows_back", "back"):
        arrays[name] = grid[name]
    arrays["own"], beside = lowering_tables()
    arrays["left"], arrays["right"] = beside
    return arrays


def whole(
    bands, size, slots, names, places, root_ref, occ_ref, kern_hbm, mask_hbm, targ_hbm, packed_hbm, low_ref, *refs
):
    count = len(names)
    held = dict(zip(names, refs[:count]))
    (kern_ref, mask_ref, targ_ref, kr_ref, ki_ref, sens_ref, out_msg, side, full, near, copy_sem, table_sem,
     side_send, side_recv, near_send, near_recv) = refs[count:]
    at = Place(bands, size)
    arrived = at.greet()
    copies = []
    pairs = [(kern_hbm, kern_ref), (targ_hbm, targ_ref)]
    piece = slots * TILE // PIECES
    for n in range(PIECES):
        span = pl.ds(n * piece, piece)
        pairs.append((mask_hbm.at[span], mask_ref.at[span]))
    for n, (src, dst) in enumerate(pairs):
        copies.append(pltpu.make_async_copy(src, dst, copy_sem.at[n]))
    mask_copies, copies = copies[2:], copies[:2]
    tables = []
    for n, (name, top, height, left, width) in enumerate(places):
        tables.append(
            pltpu.make_async_copy(
                packed_hbm.at[pl.ds(top, height), pl.ds(0, width)],
                held[name].at[:, pl.ds(left, width)],
                table_sem.at[n],
            )
        )
    early = [c for c, place in zip(tables, places) if place[0] in ("row_table", "cols")]
    late = [c for c, place in zip(tables, places) if place[0] not in ("row_table", "cols")]
    for copy in mask_copies + early + copies + late:
        copy.start()

    for copy in mask_copies + early:
        copy.wait()
    upper = mixed_dot(held["row_table"][...], mask_ref[...]).astype(jnp.bfloat16)
    half = (slots + 2) * FREQ
    three = mixed_dot(jnp.concatenate([upper[:half], upper[half:]], 1), held["cols"][...])
    first = lax.broadcasted_iota(jnp.int32, (FREQ, 128), 1) < 64

    def packed_part(dy, dx):
        def rows(tile):
            span = slice((tile + 1) * FREQ, (tile + 2) * FREQ)
            if dx == 0:
                return three[span, :128]
            value = three[span, 128:]
            turned = pltpu.roll(value, 64, 1)
            return jnp.where(first, value, turned) if dx < 0 else jnp.where(first, turned, value)

        if dy == 0:
            return jnp.where(first, rows(0), rows(1))
        return jnp.where(first, 0.0, rows(-1)) if dy < 0 else jnp.where(first, rows(slots), 0.0)

    spectrum = packed_part(0, 0)
    for n, offset in enumerate(NEAR):
        out_msg[n] = packed_part(*offset)
    arrived()

    def spread_out(sources, into, send, recv):
        sent = []
        for n, offset in enumerate(NEAR):
            there, device = at.near(*offset)
            copy = push(sources[n], into.at[n], send.at[n], recv.at[n], device)
            sent.append((there, copy))
            pl.when(there)(copy.start)
        return sent

    def take_in(sent, into):
        for n, (dy, dx) in enumerate(NEAR):
            source, _ = at.near(-dy, -dx)
            pl.when(source)(sent[n][1].wait_recv)

            @pl.when(jnp.logical_not(source))
            def _():
                into[n] = jnp.zeros((FREQ, 128), jnp.float32)

    parts_sent = spread_out([out_msg.at[n] for n in range(len(NEAR))], side, side_send, side_recv)
    copies[0].wait()
    for k in range(KERNELS):
        root = jnp.sqrt(jnp.full((1, 128), root_ref[k], jnp.float32))
        for part, ref in ((0, kr_ref), (1, ki_ref)):
            ref[k] = jnp.concatenate([kern_ref[part, k]] * 4, 1) * root
    for copy in copies[1:] + late:
        copy.wait()
    flags = [occ_ref[at.band * slots + slot, at.column] for slot in range(slots)]
    take_in(parts_sent, side)
    for n in range(len(NEAR)):
        spectrum = spectrum + side[n]
    total = spectrum_gradients(spectrum, flags, targ_ref, kr_ref, ki_ref, held, sens_ref)
    full[...] = total
    sent = spread_out([full] * len(NEAR), near, near_send, near_recv)

    def product(stack, table):
        high, low = two_parts(jnp.concatenate(stack, 0))
        table = table[...]
        return mixed_dot(jnp.concatenate([high, low], 1), jnp.concatenate([table, table], 0))

    def halves(value):
        return [jnp.where(first, value, 0.0), jnp.where(first, 0.0, value)]

    middle = product(halves(total), held["own"])
    take_in(sent, near)

    def get(dy, dx):
        return near[NEAR.index((-dy, -dx))]

    def beside(dx, table):
        outer = [jnp.where(first, 0.0, get(-1, dx)), jnp.where(first, get(1, dx), 0.0)]
        return product([outer[0]] + halves(get(0, dx)) + [outer[1]], table)

    outer = product([jnp.where(first, 0.0, get(-1, 0)), jnp.where(first, get(1, 0), 0.0)], held["own"])
    left, right = beside(-1, held["left"]), beside(1, held["right"])
    own = jnp.concatenate([outer[:FREQ], middle, outer[FREQ:]], 0)
    for part in range(2):
        value = own[:, part * TILE : (part + 1) * TILE]
        span = slice(part * 128, part * 128 + 128)
        value = jnp.concatenate(
            [value[:, :128] + left[:, span], value[:, 128:-128], value[:, -128:] + right[:, span]], 1
        ).astype(jnp.bfloat16)
        for tile in range(slots + 2):
            low_ref[(2 * tile + part) * FREQ : (2 * tile + part + 1) * FREQ, :] = value[
                tile * FREQ : (tile + 1) * FREQ
            ]
    for there, copy in parts_sent + sent:
        pl.when(there)(copy.wait_send)


def whole_call(mask_field, target_field, occupancy, kernels, weights, bands, size, slots):
    arrays = all_tables(slots)
    tables, places = packed(arrays)
    dma = pltpu.SemaphoreType.DMA
    smem, hbm = pl.BlockSpec(memory_space=pltpu.SMEM), pl.BlockSpec(memory_space=pl.ANY)
    message = pltpu.VMEM((len(NEAR), FREQ, 128), jnp.float32)
    spectra = pltpu.VMEM((KERNELS, FREQ, 128), jnp.float32)
    return pl.pallas_call(
        lambda *refs: whole(bands, size, slots, list(arrays), places, *refs),
        out_shape=jax.ShapeDtypeStruct(((slots + 2) * 2 * FREQ, TILE), jnp.bfloat16),
        in_specs=[smem, smem] + [hbm] * 4,
        out_specs=VMEM,
        scratch_shapes=[pltpu.VMEM(a.shape, jnp.bfloat16) for a in arrays.values()]
        + [
            pltpu.VMEM(kernels.shape, kernels.dtype),
            pltpu.VMEM(mask_field.shape, mask_field.dtype),
            pltpu.VMEM(target_field.shape, target_field.dtype),
            spectra, spectra,
            pltpu.VMEM((TILE, slots * TILE), jnp.bfloat16),
            message, message,
            pltpu.VMEM((FREQ, 128), jnp.float32),
            message,
            dma((2 + PIECES,)), dma((len(places),)),
            dma((len(NEAR),)), dma((len(NEAR),)), dma((len(NEAR),)), dma((len(NEAR),)),
        ],
        compiler_params=pltpu.CompilerParams(
            collective_id=0, has_side_effects=True, vmem_limit_bytes=VMEM_GRANT
        ),
    )(weights, occupancy, kernels, mask_field, target_field, jnp.asarray(tables))


def finish_call(lowered, mask_field, slots):
    table = jnp.asarray(np.ascontiguousarray(spread(slots).T))
    height, width = mask_field.shape
    rows = 256
    steps = height // rows

    def finish(table_ref, low_ref, mask_ref, out_ref, held, sems):
        copies = []
        for step in range(steps):
            span = pl.ds(step * rows, rows)
            values = mask_ref[span, :].astype(jnp.float32)
            penalty = GAMMA * 4.0 * values * (values * values - 1.0)
            held[span, :] = mixed_dot(table_ref[span, :], low_ref[...]) + penalty
            copies.append(pltpu.make_async_copy(held.at[span], out_ref.at[span], sems.at[step]))
            copies[-1].start()
        for copy in copies:
            copy.wait()

    return pl.pallas_call(
        finish,
        out_shape=jax.ShapeDtypeStruct((height, width), jnp.float32),
        in_specs=[VMEM, VMEM, VMEM],
        out_specs=pl.BlockSpec(memory_space=pl.ANY),
        scratch_shapes=[pltpu.VMEM((height, width), jnp.float32), pltpu.SemaphoreType.DMA((steps,))],
        compiler_params=pltpu.CompilerParams(vmem_limit_bytes=16 * 1024 * 1024),
    )(table, lowered, mask_field)


def on_device(mask_field, target_field, occupancy, kernels, weights):
    slots = mask_field.shape[0] // TILE
    bands, size = lax.axis_size("own"), lax.axis_size("img")
    assert slots == 2
    lowered = whole_call(mask_field, target_field, occupancy, kernels, weights, bands, size, slots)
    return finish_call(lowered, mask_field, slots)


def solution(mesh):
    return jax.shard_map(
        on_device,
        mesh=mesh,
        in_specs=(P("own", "img"), P("own", "img"), P(), P(), P()),
        out_specs=P("own", "img"),
        check_vma=False,
    )
```
